32 devices in a mesh: expert: 8 (over y, x, core), dp: 4 (over z).
Axes of the slice: x: 2, y: 2, z: 4, core: 2. Of those that a mesh axis runs over, the one named last changes fastest.
Arguments:
- rows_x: bfloat16 [2048, 4096], P('expert'), may hold values from -6 to 6
- rows_dy: bfloat16 [2048, 4096], P('expert'), may hold values from -2 to 2
- router_logits: float32 [2048, 8], P('expert'), may hold values from -7.5 to 307.5
- expert_of: int32 [2048, 1], P('expert'), may hold values from 0 to 7, as said below
- w_gate: bfloat16 [8, 1536, 4096], P('expert', 'dp'), may hold values from -0.09375 to 0.09375
- w_up: bfloat16 [8, 1536, 4096], P('expert', 'dp'), may hold values from -0.09375 to 0.09375
- w_down: bfloat16 [8, 1536, 4096], P('expert', 'dp'), may hold values from -0.15625 to 0.15625
Outputs:
- grad_rows: bfloat16 [2048, 4096], P('expert', 'dp')
- grad_logits: float32 [2048, 8], P('expert')
- grad_gate: float32 [8, 1536, 4096], P('expert', 'dp')
- grad_up: float32 [8, 1536, 4096], P('expert', 'dp')
- grad_down: float32 [8, 1536, 4096], P('expert', 'dp')
- grad_norm: float32 [], replicated
The draws below stay inside these ranges and needn't reach their ends.
Inputs may be any that keep to these rules, and one draw needn't show every extreme that they name: `expert_of`: one expert, the same in every aligned block of 256 rows, is named by exactly 64 rows of each block; a second expert, the same in every block, by exactly 32 rows of each block; every other expert by at most 32 rows of a block.
All inputs are finite; a program needn't handle non-finite values.
Results may differ from the reference program's by a relative error of at most 0.015.
Values may be sent and summed in bfloat16 or wider, within the bound.
No kernel may reach another device: no remote copies, remote signals or barrier semaphores. Data moves between devices by JAX's collectives and lax.ppermute only.
A program may use at most 192 MiB of HBM per device.

```python
from functools import partial
import jax
import jax.numpy as jnp
from jax import lax

D = 4096
FF = 1536
R_DEV = 256
HOT = 1
EXPERTS = 8
CAP = 64
COLD_CAP = 32
ROWS = 2048
N_DP = 4


def draw_router_logits(key, part):
    base_key = jax.random.fold_in(jax.random.fold_in(key, 71), 0)
    scores = jnp.clip(1.5 * jax.random.normal(base_key, (ROWS, EXPERTS), jnp.float32), -7.5, 7.5)
    return scores


def draw_expert_of(key, part):
    base_key = jax.random.fold_in(key, 29)
    hot_key, full_key, block_key = jax.random.split(base_key, 3)
    hot_expert = jax.random.randint(hot_key, (), 0, EXPERTS).astype(jnp.int32)
    full_cold = jax.random.randint(full_key, (), 0, EXPERTS - 1).astype(jnp.int32)
    cold_slots = (EXPERTS - 1) * COLD_CAP
    cold_rows = R_DEV - CAP
    owner = jnp.repeat(jnp.arange(EXPERTS - 1, dtype=jnp.int32), COLD_CAP, total_repeat_length=cold_slots)

    def one_block(block_seed):
        pick_key, order_key = jax.random.split(block_seed)
        rank_key = jax.random.permutation(pick_key, cold_slots).astype(jnp.int32)
        priority = jnp.where(owner == full_cold, -1, rank_key)
        chosen = owner[jnp.argsort(priority, stable=True)[:cold_rows]]
        chosen = chosen + (chosen >= hot_expert).astype(jnp.int32)
        block = jnp.concatenate([jnp.full((CAP,), hot_expert, jnp.int32), chosen])
        return jax.random.permutation(order_key, block)
    blocks = jax.vmap(one_block)(jax.random.split(block_key, ROWS // R_DEV))
    return blocks.reshape(ROWS, 1).astype(jnp.int32)


def shard_levels(rng, shape, pieces, smallest, high):
    loudness = 1.0
    for axis_at, shards_of in pieces:
        steps = jax.random.uniform(jax.random.fold_in(jax.random.fold_in(rng, 6), axis_at), (shards_of,), jnp.float32, smallest / len(pieces), high / len(pieces))
        loudness = loudness * jnp.repeat(jnp.exp(steps), shape[axis_at] // shards_of).reshape((-1,) + (1,) * (len(shape) - 1 - axis_at))
    return loudness


def scatter_about(key, extent, deviation, limit, cuts=(), held_as=jnp.bfloat16):
    entries = jax.random.normal(key, extent, jnp.float32) * deviation
    if len(cuts) > 0:
        entries = shard_levels(key, extent, cuts, -0.22, 0.18) * entries
    return jnp.clip(entries, min=-limit, max=limit).astype(held_as)


def setup_inputs(seed: int = 0) -> dict:
    keys = jax.random.split(jax.random.key(seed), 8)
    return {
        "rows_x": scatter_about(keys[0], (ROWS, D), 1.0, 6.0, ((0, 8),)),
        "rows_dy": scatter_about(keys[1], (ROWS, D), 0.25, 2.0, ((0, 8),)),
        "router_logits": draw_router_logits(jax.random.fold_in(keys[7], 71), 0),
        "expert_of": draw_expert_of(jax.random.fold_in(keys[7], 71), 0),
        "w_gate": scatter_about(keys[4], (EXPERTS, FF, D), D ** -0.5, 0.09375, ((0, 8), (1, 4))),
        "w_up": scatter_about(keys[5], (EXPERTS, FF, D), D ** -0.5, 0.09375, ((0, 8), (1, 4))),
        "w_down": scatter_about(keys[6], (EXPERTS, FF, D), FF ** -0.5, 0.15625, ((0, 8), (1, 4))),
    }


aux_weight = 1.0

def rank_rows(expert_ids):
    onehot = (expert_ids[:, None] == jnp.arange(EXPERTS, dtype=jnp.int32)[None, :]).astype(jnp.int32)
    earlier = jnp.cumsum(onehot, axis=0) - onehot
    return lax.optimization_barrier(jnp.sum(earlier * onehot, axis=1)).astype(jnp.int32)

def place_rows(values, target, total):
    return jnp.zeros((total,) + values.shape[1:], values.dtype).at[target].set(values, mode='drop')

def take_rows(values, target):
    return values[jnp.minimum(target, values.shape[0] - 1)]

def expert_backward(rows_in, grads_in, gates_in, gate_weight, up_weight, down_weight):
    scaled = (gates_in.astype(jnp.float32)[:, None] * grads_in.astype(jnp.float32)).astype(jnp.bfloat16)
    gate_pre = lax.dot_general(rows_in, gate_weight, (((1,), (1,)), ((), ())), preferred_element_type=jnp.float32)
    up_pre = lax.dot_general(rows_in, up_weight, (((1,), (1,)), ((), ())), preferred_element_type=jnp.float32)
    sigmoid_gate = jax.nn.sigmoid(gate_pre)
    active = gate_pre * sigmoid_gate
    hidden = (active * up_pre).astype(jnp.bfloat16)
    output_part = jnp.dot(hidden, down_weight, preferred_element_type=jnp.float32)
    gate_part = lax.optimization_barrier(jnp.sum(grads_in.astype(jnp.float32) * output_part, axis=1))
    grad_hidden = lax.dot_general(scaled, down_weight, (((1,), (1,)), ((), ())), preferred_element_type=jnp.float32)
    grad_upper = (grad_hidden * active).astype(jnp.bfloat16)
    grad_pre = (grad_hidden * up_pre * sigmoid_gate * (1.0 + gate_pre * (1.0 - sigmoid_gate))).astype(jnp.bfloat16)
    down_grad_t = lax.dot_general(scaled, hidden, (((0,), (0,)), ((), ())), preferred_element_type=jnp.float32)
    gate_grad_w = lax.dot_general(grad_pre, rows_in, (((0,), (0,)), ((), ())), preferred_element_type=jnp.float32)
    up_grad_w = lax.dot_general(grad_upper, rows_in, (((0,), (0,)), ((), ())), preferred_element_type=jnp.float32)
    input_part = jnp.dot(grad_pre, gate_weight, preferred_element_type=jnp.float32)
    input_part = input_part + jnp.dot(grad_upper, up_weight, preferred_element_type=jnp.float32)
    rounded = lax.optimization_barrier(input_part.astype(jnp.bfloat16)).astype(jnp.float32)
    return (rounded, gate_part, gate_grad_w, up_grad_w, down_grad_t)

def one_expert(operands):
    rows_in, grads_in, gates_in, gate_weight, up_weight, down_weight = operands
    hidden_shard = FF // N_DP
    input_acc = jnp.zeros((rows_in.shape[0], D), jnp.float32)
    gate_acc = jnp.zeros((rows_in.shape[0],), jnp.float32)
    gate_list, up_list, down_list = ([], [], [])
    for shard_index in range(N_DP):
        row_start = shard_index * hidden_shard
        row_end = row_start + hidden_shard
        result = expert_backward(rows_in, grads_in, gates_in, gate_weight[row_start:row_end, :], up_weight[row_start:row_end, :], down_weight[row_start:row_end, :])
        input_acc = input_acc + result[0]
        gate_acc = gate_acc + result[1]
        gate_list.append(result[2])
        up_list.append(result[3])
        down_list.append(result[4].T)
    return (input_acc.astype(jnp.bfloat16), gate_acc.astype(jnp.bfloat16), jnp.concatenate(gate_list, axis=0), jnp.concatenate(up_list, axis=0), jnp.concatenate(down_list, axis=0))

def reference(rows_x, rows_dy, router_logits, expert_of, w_gate, w_up, w_down):
    blocks = ROWS // R_DEV
    router_probs = jax.nn.softmax(router_logits, axis=1)
    expert_ids = expert_of[:, 0]
    expert_iota = jnp.arange(EXPERTS, dtype=jnp.int32)
    onehot_int = (expert_ids[:, None] == expert_iota[None, :]).astype(jnp.int32)
    onehot_all = onehot_int.astype(jnp.float32)
    counts = lax.optimization_barrier(jnp.sum(onehot_int, axis=0))
    gate_b = lax.optimization_barrier(jnp.sum(router_probs * onehot_all, axis=1)).astype(jnp.bfloat16)
    scores = counts * EXPERTS + (EXPERTS - 1 - expert_iota)
    hot_ids = lax.top_k(scores, HOT)[1].astype(jnp.int32)
    block_ids = expert_ids.reshape(blocks, R_DEV)
    ranking = jax.vmap(rank_rows)(block_ids)
    row_hot = jnp.any(block_ids[:, :, None] == hot_ids[None, None, :], axis=2)
    cold_total = EXPERTS * COLD_CAP
    cold_target = jnp.where(row_hot, cold_total, block_ids * COLD_CAP + ranking).astype(jnp.int32)
    block_rows = rows_x.reshape(blocks, R_DEV, D)
    block_grads = rows_dy.reshape(blocks, R_DEV, D)
    block_gates = gate_b.reshape(blocks, R_DEV)
    place_cold = jax.vmap(partial(place_rows, total=cold_total))
    cold_rows = place_cold(block_rows, cold_target).reshape(blocks, EXPERTS, COLD_CAP, D).transpose(1, 0, 2, 3).reshape(EXPERTS, blocks * COLD_CAP, D)
    cold_grads = place_cold(block_grads, cold_target).reshape(blocks, EXPERTS, COLD_CAP, D).transpose(1, 0, 2, 3).reshape(EXPERTS, blocks * COLD_CAP, D)
    cold_gates = place_cold(block_gates, cold_target).reshape(blocks, EXPERTS, COLD_CAP).transpose(1, 0, 2).reshape(EXPERTS, blocks * COLD_CAP)
    results = lax.map(one_expert, (cold_rows, cold_grads, cold_gates, w_gate, w_up, w_down))
    grad_gate, grad_up, grad_down = (results[2], results[3], results[4])
    back_cold = results[0].reshape(EXPERTS, blocks, COLD_CAP, D).transpose(1, 0, 2, 3).reshape(blocks, cold_total, D)
    back_cold_gates = results[1].reshape(EXPERTS, blocks, COLD_CAP).transpose(1, 0, 2).reshape(blocks, cold_total)
    grad_rows = jax.vmap(take_rows)(back_cold, cold_target)
    gate_rows = jax.vmap(take_rows)(back_cold_gates, cold_target)
    place_hot = jax.vmap(partial(place_rows, total=CAP))
    for hot_index in range(HOT):
        hot_id = hot_ids[hot_index]
        on_hot = block_ids == hot_id
        hot_target = jnp.where(on_hot, ranking, CAP).astype(jnp.int32)
        hot_rows = place_hot(block_rows, hot_target).reshape(blocks * CAP, D)
        hot_grads = place_hot(block_grads, hot_target).reshape(blocks * CAP, D)
        hot_gates = place_hot(block_gates, hot_target).reshape(blocks * CAP)
        hot_result = one_expert((hot_rows, hot_grads, hot_gates, w_gate[hot_id], w_up[hot_id], w_down[hot_id]))
        grad_gate = grad_gate.at[hot_id].add(hot_result[2])
        grad_up = grad_up.at[hot_id].add(hot_result[3])
        grad_down = grad_down.at[hot_id].add(hot_result[4])
        hot_back = hot_result[0].reshape(blocks, CAP, D)
        hot_back_gates = hot_result[1].reshape(blocks, CAP)
        grad_rows = jnp.where(on_hot[:, :, None], jax.vmap(take_rows)(hot_back, hot_target), grad_rows)
        gate_rows = jnp.where(on_hot, jax.vmap(take_rows)(hot_back_gates, hot_target), gate_rows)
    grad_rows = grad_rows.reshape(ROWS, D)
    gate_rows = gate_rows.reshape(ROWS).astype(jnp.float32)
    fractions = counts.astype(jnp.float32) / ROWS
    pulls = onehot_all * gate_rows[:, None] + aux_weight * EXPERTS * fractions[None, :]
    grad_logits = router_probs * (pulls - lax.optimization_barrier(jnp.sum(router_probs * pulls, axis=1, keepdims=True)))
    squares = jnp.sum(grad_gate * grad_gate) + jnp.sum(grad_up * grad_up) + jnp.sum(grad_down * grad_down)
    return (grad_rows, grad_logits, grad_gate, grad_up, grad_down, jnp.sqrt(squares))
```

```python
import functools

import jax
import jax.numpy as jnp
from jax import lax
from jax.experimental import pallas as pl
from jax.experimental.pallas import tpu as pltpu
from jax.sharding import PartitionSpec as P

aux_weight = 1.0
LANES = 128
COUNT_LANE = 64
BF16 = jnp.bfloat16
F32 = jnp.float32
ANY = pl.BlockSpec(memory_space=pl.ANY)
VMEM = pl.BlockSpec(memory_space=pltpu.VMEM)
SMEM = pl.BlockSpec(memory_space=pltpu.SMEM)


def call(body, name, out_shape, in_specs, out_specs, scratch, micros, room, **extra):
    return pl.pallas_call(
        body,
        name=name,
        out_shape=out_shape,
        in_specs=in_specs,
        out_specs=out_specs,
        scratch_shapes=scratch,
        cost_estimate=pl.CostEstimate(
            flops=int(micros * 5e7), bytes_accessed=int(micros * 1e5), transcendentals=0
        ),
        compiler_params=pltpu.CompilerParams(vmem_limit_bytes=room * 1024 * 1024),
        **extra,
    )


def lane_iota(shape):
    return lax.broadcasted_iota(jnp.int32, shape, len(shape) - 1)


def routing(ids, me, cap, experts):
    rows = ids.shape[1]
    expert = lax.broadcasted_iota(jnp.int32, (experts, rows), 0)
    onehot = jnp.where(expert == ids, 1.0, 0.0)
    before = lax.broadcasted_iota(jnp.int32, (rows, rows), 0) < lane_iota((rows, rows))
    earlier = jnp.dot(
        onehot.astype(BF16), jnp.where(before, 1.0, 0.0).astype(BF16), preferred_element_type=F32
    )
    rank = jnp.sum(earlier * onehot, axis=0, keepdims=True).astype(jnp.int32)
    slot = jnp.where(rank < cap, (ids ^ me) * cap + rank, experts * cap + rank - cap)
    slots = -(-(experts + 1) * cap // LANES) * LANES
    spread = lax.broadcasted_iota(jnp.int32, (slots, rows), 0) == slot
    return onehot, jnp.where(spread, 1.0, 0.0)


def softmax(logits):
    scores = jnp.exp(logits - jnp.max(logits, axis=0, keepdims=True))
    return scores / jnp.sum(scores, axis=0, keepdims=True)


def dispatch_body(experts, cap, width, place, x_hbm, dy_hbm, logits, ids, *refs):
    outs, hot = refs[: experts + 1], refs[experts + 1]
    held, sent, in_sems, out_sems = refs[experts + 2 :]
    loads = [
        pltpu.make_async_copy(source, held.at[:, pl.ds(i * width, width)], in_sems.at[i])
        for i, source in enumerate((x_hbm, dy_hbm))
    ]
    for load in loads:
        load.start()
    me = place[0]
    expert_ids = ids[...]
    slots = sent.shape[0]
    onehot, spread = routing(expert_ids, me, cap, experts)
    spread = spread[:slots]
    gate = jnp.sum(softmax(logits[...]) * onehot, axis=0, keepdims=True)
    gate = gate.astype(BF16).astype(F32)
    mine = jnp.sum(jnp.where(expert_ids == me, 1, 0))
    hot[0] = jnp.where(mine > cap, 1, 0)
    counts = jnp.sum(onehot, axis=1, keepdims=True)
    expert = lax.broadcasted_iota(jnp.int32, (experts, LANES), 0)
    counts = jnp.sum(
        jnp.where(lane_iota((experts, LANES)) - COUNT_LANE == expert, counts, 0.0),
        axis=0,
        keepdims=True,
    )
    gates = jnp.sum(spread * gate, axis=1, keepdims=True)
    sent[:, 2 * width :] = jnp.where(lane_iota((slots, LANES)) == 0, gates, counts).astype(BF16)
    spread = spread.astype(BF16)
    stores = []
    tile = 1024
    for half in range(2):
        loads[half].wait()
        for at in range(half * width, (half + 1) * width, tile):
            sent[:, at : at + tile] = jnp.dot(
                spread, held[:, at : at + tile], preferred_element_type=F32
            ).astype(BF16)
        size = width if half == 0 else width + LANES
        for m in range(experts + 1):
            store = pltpu.make_async_copy(
                sent.at[pl.ds(m * cap, cap), pl.ds(half * width, size)],
                outs[m].at[:, pl.ds(half * width, size)],
                out_sems.at[half, m],
            )
            store.start()
            stores.append(store)
    for store in stores:
        store.wait()


def dispatch(place, rows_x, rows_dy, logits, ids, experts, cap):
    rows, width = rows_x.shape
    wide = 2 * width + LANES
    slots = (experts + 1) * cap
    return call(
        functools.partial(dispatch_body, experts, cap, width),
        "dispatch",
        [jax.ShapeDtypeStruct((cap, wide), BF16)] * (experts + 1)
        + [jax.ShapeDtypeStruct((1,), jnp.int32)],
        [SMEM, ANY, ANY, VMEM, VMEM],
        [ANY] * (experts + 1) + [SMEM],
        [
            pltpu.VMEM((rows, 2 * width), BF16),
            pltpu.VMEM((slots, wide), BF16),
            pltpu.SemaphoreType.DMA((2,)),
            pltpu.SemaphoreType.DMA((2, experts + 1)),
        ],
        6,
        16,
    )(place, rows_x, rows_dy, logits, ids)


def split_lanes(total):
    lane = lane_iota((total.shape[0], LANES))
    first = total.astype(BF16).astype(F32)
    second = (total - first).astype(BF16).astype(F32)
    third = total - first - second
    return jnp.where(
        lane == 0, first, jnp.where(lane == 1, second, jnp.where(lane == 2, third, 0.0))
    ).astype(BF16)


def rows_body(pieces, cap, width, n_dp, guarded, place, hot, *refs):
    sources, weights = refs[:pieces], refs[pieces : pieces + 3]
    outs = refs[pieces + 3 : -2]
    held, piece_sems = refs[-2:]
    hidden_units = weights[0].shape[0]
    rows = held.shape[0]

    def work():
        copies = [
            pltpu.make_async_copy(
                sources[p], held.at[pl.ds(p * cap, cap), :], piece_sems.at[p]
            )
            for p in range(pieces)
        ]
        for copy in copies:
            copy.start()
        for copy in copies:
            copy.wait()
        pre_gate, pre_up, grad = [
            lax.dot_general(
                held[:, side * width : (side + 1) * width],
                weight[...],
                (((1,), (1,)), ((), ())),
                preferred_element_type=F32,
            )
            for side, weight in zip((0, 0, 1), weights)
        ]
        gate = held[:, 2 * width :].astype(F32)[:, 0:1]
        sigmoid = jax.nn.sigmoid(pre_gate)
        active = pre_gate * sigmoid
        hidden = (active * pre_up).astype(BF16)
        hidden_f = hidden.astype(F32)
        gate_part = jnp.sum(hidden_f * grad, axis=1, keepdims=True)
        grad_hidden = grad * gate
        d_up = (grad_hidden * active).astype(BF16)
        d_pre = (grad_hidden * pre_up * sigmoid * (1.0 + pre_gate * (1.0 - sigmoid))).astype(BF16)
        outs[-1][:, :hidden_units] = d_pre
        outs[-1][:, hidden_units : 2 * hidden_units] = d_up
        outs[-1][:, 2 * hidden_units :] = (hidden_f * gate).astype(BF16)
        part = split_lanes(gate_part)
        cut = width // n_dp
        me = place[1]
        halves = 2 if not guarded else 4
        for half in range(halves):
            first = 0 if half < 2 else rows // 2
            size = rows if not guarded else rows // 2
            outs[half][:, n_dp // 2 * cut :] = part[first : first + size]
            for p in range(n_dp // 2):
                column = pl.multiple_of((me ^ (2 * p + half % 2)) * cut, cut)
                outs[half][:, p * cut : (p + 1) * cut] = (
                    jnp.dot(
                        d_pre[first : first + size],
                        weights[0][:, pl.ds(column, cut)],
                        preferred_element_type=F32,
                    )
                    + jnp.dot(
                        d_up[first : first + size],
                        weights[1][:, pl.ds(column, cut)],
                        preferred_element_type=F32,
                    )
                ).astype(BF16)

    if guarded:

        @pl.when(hot[0] == 1)
        def _():
            work()

        @pl.when(hot[0] != 1)
        def _():
            for out in outs:
                out[...] = jnp.zeros_like(out)
    else:
        work()


def rows_backward(place, hot, sources, weights, cap, n_dp, guarded):
    width = weights[0].shape[1]
    hidden_units = weights[0].shape[0]
    pieces = len(sources)
    rows = pieces * cap
    part = width // 2 + LANES
    parts = [(rows, part)] * 2 if not guarded else [(rows // 2, part)] * 4
    return call(
        functools.partial(rows_body, pieces, cap, width, n_dp, guarded),
        "rows_backward",
        [jax.ShapeDtypeStruct(s, BF16) for s in parts]
        + [jax.ShapeDtypeStruct((rows, 3 * hidden_units), BF16)],
        [SMEM, SMEM] + [ANY] * pieces + [VMEM] * 3,
        [VMEM] * (len(parts) + 1),
        [
            pltpu.VMEM((rows, 2 * width + LANES), BF16),
            pltpu.SemaphoreType.DMA((pieces,)),
        ],
        7,
        20,
    )(place, hot, *sources, *weights)


def merge_body(*refs):
    count = len(refs) // 3
    for a, b, out in zip(refs[:count], refs[count : 2 * count], refs[2 * count :]):
        out[...] = a[...] + b[...]


def merge(own, peers):
    return call(
        merge_body,
        "merge",
        [jax.ShapeDtypeStruct(a.shape, a.dtype) for a in own],
        [VMEM] * (2 * len(own)),
        [VMEM] * len(own),
        [],
        2,
        8,
    )(*own, *peers)


def fold_body(cut, parts, cap, kept, got, *outs):
    gate_part = jnp.sum(
        kept[:, parts * cut :].astype(F32) + got[:, parts * cut :].astype(F32),
        axis=1,
        keepdims=True,
    )
    lanes = split_lanes(gate_part)
    if parts == 1:
        total = kept[:, :cut].astype(F32) + got[:, :cut].astype(F32)
        for p, out in enumerate(outs):
            out[:, :cut] = total[p * cap : (p + 1) * cap].astype(BF16)
            out[:, cut:] = lanes[p * cap : (p + 1) * cap]
        return
    for out in outs:
        out[:, parts // 2 * cut :] = lanes
    for p in range(parts):
        total = kept[:, p * cut : (p + 1) * cut].astype(F32) + got[
            :, p * cut : (p + 1) * cut
        ].astype(F32)
        outs[p % 2][:, p // 2 * cut : (p // 2 + 1) * cut] = total.astype(BF16)


def fold(kept, got, cut, parts, cap):
    rows = kept.shape[0]
    if parts == 1:
        shapes = [(cap, cut + LANES)] * (rows // cap)
    else:
        shapes = [(rows, parts // 2 * cut + LANES)] * 2
    return call(
        functools.partial(fold_body, cut, parts, cap),
        "fold",
        [jax.ShapeDtypeStruct(s, BF16) for s in shapes],
        [VMEM, VMEM],
        [VMEM] * len(shapes),
        [],
        2,
        8,
    )(kept, got)


def weights_body(cold_pieces, hot_pieces, acts_count, cap, width, tile, hot, *refs):
    pieces = cold_pieces + hot_pieces
    sources, acts = refs[:pieces], refs[pieces : pieces + acts_count]
    outs, squares = refs[pieces + acts_count : -4][:3], refs[pieces + acts_count : -4][3]
    held, factors, total, sems = refs[-4:]
    step = pl.program_id(0)
    hidden_units = outs[0].shape[0]
    cold_rows = cold_pieces * cap

    def copies(count):
        return [
            pltpu.make_async_copy(
                sources[p].at[:, pl.ds(0, 2 * width)],
                held.at[pl.ds(p * cap, cap), :],
                sems.at[p],
            )
            for p in count
        ]

    @pl.when(step == 0)
    def _():
        for copy in copies(range(cold_pieces)):
            copy.start()

        @pl.when(hot[0] == 1)
        def _():
            for copy in copies(range(cold_pieces, pieces)):
                copy.start()

        at = 0
        for act in acts:
            factors[:, at : at + act.shape[0]] = act[...].astype(F32).T.astype(BF16)
            at += act.shape[0]
        total[...] = jnp.zeros_like(total)
        for copy in copies(range(cold_pieces)):
            copy.wait()

        @pl.when(hot[0] == 1)
        def _():
            for copy in copies(range(cold_pieces, pieces)):
                copy.wait()

    def work(rows):
        for i in range(3):
            at = pl.multiple_of((width if i == 2 else 0) + step * tile, tile)
            gradient = jnp.dot(
                factors[i * hidden_units : (i + 1) * hidden_units, :rows],
                held[:rows, pl.ds(at, tile)],
                preferred_element_type=F32,
            )
            outs[i][...] = gradient
            total[...] += jnp.sum((gradient * gradient).reshape(-1, 8, tile), axis=0)

    @pl.when(hot[0] == 1)
    def _():
        work(pieces * cap)

    @pl.when(hot[0] != 1)
    def _():
        work(cold_rows)

    @pl.when(step == pl.num_programs(0) - 1)
    def _():
        squares[...] = jnp.full(squares.shape, jnp.sum(total[...]), F32)


def weights_backward(hot, cold, extra, acts, hidden_units, width, cap):
    tile = 512
    rows = (len(cold) + len(extra)) * cap
    block = pl.BlockSpec((hidden_units, tile), lambda j: (0, j))
    whole = [pl.BlockSpec(a.shape, lambda j: (0, 0)) for a in acts]
    return call(
        functools.partial(
            weights_body, len(cold), len(extra), len(acts), cap, width, tile
        ),
        "weights_backward",
        [jax.ShapeDtypeStruct((hidden_units, width), F32)] * 3
        + [jax.ShapeDtypeStruct((8, LANES), F32)],
        [SMEM] + [ANY] * (len(cold) + len(extra)) + whole,
        [block] * 3 + [pl.BlockSpec((8, LANES), lambda j: (0, 0))],
        [
            pltpu.VMEM((rows, 2 * width), BF16),
            pltpu.VMEM((3 * hidden_units, rows), BF16),
            pltpu.VMEM((8, tile), F32),
            pltpu.SemaphoreType.DMA((len(cold) + len(extra),)),
        ],
        13,
        24,
        grid=(width // tile,),
    )(hot, *cold, *extra, *acts)


def home_body(experts, cap, cut, row_total, place, logits, ids, *refs):
    arrived, back, extra = refs[:experts], refs[experts : 2 * experts], refs[2 * experts : -5]
    grad_rows, grad_logits, pads, table, sems = refs[-5:]
    copies = [
        pltpu.make_async_copy(
            arrived[m].at[pl.ds(0, 16), pl.ds(arrived[m].shape[1] - LANES, LANES)],
            pads.at[pl.ds(16 * m, 16), :],
            sems.at[m],
        )
        for m in range(experts)
    ]
    for copy in copies:
        copy.start()
    onehot, spread = routing(ids[...], place[0], cap, experts)
    slots = (experts + 1) * cap
    for m in range(experts):
        table[m * cap : (m + 1) * cap, :] = back[m][...]
    over = extra[0][...]
    for piece in extra[1:]:
        over = over + piece[...]
    table[experts * cap :, :] = over
    pick = spread.T[:, :slots].astype(BF16)
    grad_rows[...] = jnp.dot(pick, table[:, :cut], preferred_element_type=F32).astype(BF16)
    gate_rows = jnp.dot(pick, table[:, cut:], preferred_element_type=F32).T[0:1]
    for copy in copies:
        copy.wait()
    counts = jnp.zeros((1, LANES), F32)
    for m in range(experts):
        counts = counts + pads[16 * m : 16 * m + 16, :].astype(F32)[0:1]
    counts = jnp.broadcast_to(counts, (8, LANES)).T[COUNT_LANE : COUNT_LANE + experts, 0:1]
    probs = softmax(logits[...])
    pulls = onehot * gate_rows + aux_weight * experts * (counts / row_total)
    grad_logits[...] = probs * (pulls - jnp.sum(probs * pulls, axis=0, keepdims=True))


def home(place, logits, ids, arrived, back, extra, cap, row_total):
    experts = len(back)
    rows = ids.shape[1]
    cut = back[0].shape[1] - LANES
    return call(
        functools.partial(home_body, experts, cap, cut, row_total),
        "home",
        [
            jax.ShapeDtypeStruct((rows, cut), BF16),
            jax.ShapeDtypeStruct(logits.shape, F32),
        ],
        [SMEM, VMEM, VMEM] + [ANY] * experts + [VMEM] * (experts + len(extra)),
        [VMEM, VMEM],
        [
            pltpu.VMEM((16 * experts, LANES), BF16),
            pltpu.VMEM(((experts + 1) * cap, cut + LANES), BF16),
            pltpu.SemaphoreType.DMA((experts,)),
        ],
        4,
        8,
    )(place, logits, ids, *arrived, *back, *extra)


def swap(value, axis, mask):
    size = lax.axis_size(axis)
    return lax.ppermute(value, axis, [(i, i ^ mask) for i in range(size)])


def after(value, *done):
    return lax.optimization_barrier((value, *done))[0]


def groups_of(experts):
    order = {}
    for m in range(2, experts):
        order.setdefault((bin(m >> 1).count("1"), m & 1), []).append(m)
    return [order[key] for key in sorted(order)]


def local(rows_x, rows_dy, router_logits, expert_of, w_gate, w_up, w_down):
    experts = lax.axis_size("expert")
    n_dp = lax.axis_size("dp")
    rows, width = rows_x.shape
    cap = rows // 8
    cut = width // n_dp
    place = jnp.stack([lax.axis_index("expert"), lax.axis_index("dp")]).astype(jnp.int32)
    weights = (w_gate[0], w_up[0], w_down[0])
    hidden_units = weights[0].shape[0]
    logits, ids = router_logits.T, expert_of.reshape(1, rows)
    *pieces, spare, hot = dispatch(place, rows_x, rows_dy, logits, ids, experts, cap)

    evens = list(range(0, experts, 2))
    odds = list(range(1, experts, 2))
    groups = groups_of(experts)
    cold = {0: pieces[0], 1: swap(pieces[1], "expert", 1)}
    extra = {0: spare, 1: swap(spare, "expert", 1)}
    sends = [(extra, list(level)) for level in groups[::2]] + [(cold, g) for g in groups]
    done = []
    for i, (held, group) in enumerate(sends):
        for m in group:
            piece = spare if held is extra else pieces[m]
            if i >= 2:
                piece = after(piece, *done[i - 2])
            held[m] = swap(piece, "expert", m)
        done.append([held[m] for m in group])
        if held is extra:
            for m in group:
                extra[m ^ 1] = swap(extra[m], "expert", 1)

    def along_dp(kept, sent):
        step = 1
        while True:
            got = swap(sent, "dp", step)
            parts = (kept.shape[1] - LANES) // cut
            if parts == 1:
                return fold(kept, got, cut, 1, cap)
            kept, sent = fold(kept, got, cut, parts, cap)
            step *= 2

    *parts, acts_hot = rows_backward(
        place, hot, [extra[m] for m in evens + odds], weights, cap, n_dp, True
    )
    peers = [swap(part, "expert", 1) for part in parts[2:]]
    kept, sent = merge(parts[:2], peers)
    extra_back = along_dp(kept, sent)
    back_extra = [extra_back[0]]
    for i, m in enumerate(evens[1:]):
        back_extra.append(swap(extra_back[1 + i], "expert", m))

    chunks = [[0, 1] + groups[0], groups[1], sum(groups[2:], [])]
    acts, back = [], {}
    last = acts_hot
    for chunk in chunks:
        kept, sent, act = rows_backward(
            place, after(hot, last), [cold[m] for m in chunk], weights, cap, n_dp, False
        )
        acts.append(act)
        last = act
        for m, piece in zip(chunk, along_dp(kept, sent)):
            back[m] = piece if m == 0 else swap(piece, "expert", m)

    masks = [m for chunk in chunks for m in chunk]
    grad_gate, grad_up, grad_down, squares = weights_backward(
        hot,
        [cold[m] for m in masks],
        [extra[m] for m in evens + odds],
        acts + [acts_hot],
        hidden_units,
        width,
        cap,
    )
    squares = squares + swap(squares, "expert", 1)
    squares = squares + sum(swap(squares, "dp", m) for m in range(1, n_dp))
    squares = squares + sum(swap(squares, "expert", m) for m in evens[1:])
    grad_rows, grad_logits = home(
        place,
        logits,
        ids,
        [cold[m] for m in range(experts)],
        [back[m] for m in range(experts)],
        back_extra,
        cap,
        rows * experts,
    )
    return (
        grad_rows,
        grad_logits.T,
        grad_gate[None],
        grad_up[None],
        grad_down[None],
        jnp.sqrt(squares[0, 0]),
    )


def solution(mesh):
    in_specs = (
        P("expert", None),
        P("expert", None),
        P("expert", None),
        P("expert", None),
        P("expert", "dp", None),
        P("expert", "dp", None),
        P("expert", "dp", None),
    )
    out_specs = (
        P("expert", "dp"),
        P("expert", None),
        P("expert", "dp", None),
        P("expert", "dp", None),
        P("expert", "dp", None),
        P(),
    )
    return jax.shard_map(local, mesh=mesh, in_specs=in_specs, out_specs=out_specs, check_vma=False)
```

```python
import functools

import jax
import jax.numpy as jnp
from jax import lax
from jax.experimental import pallas as pl
from jax.experimental.pallas import tpu as pltpu
from jax.sharding import PartitionSpec as P

aux_weight = 1.0
LANES = 128
COUNT_LANE = 64
RATE = 1e9
SQUARE_LANE = 8
BF16 = jnp.bfloat16
F32 = jnp.float32
ANY = pl.BlockSpec(memory_space=pl.ANY)
VMEM = pl.BlockSpec(memory_space=pltpu.VMEM)
SMEM = pl.BlockSpec(memory_space=pltpu.SMEM)
HBM = pl.BlockSpec(memory_space=pltpu.HBM)


def call(body, name, out_shape, in_specs, out_specs, scratch, micros, room, earlier=(), **extra):
    skipped = len(earlier)

    def without(*refs):
        body(*refs[skipped:])

    kernel = pl.pallas_call(
        without,
        name=name,
        out_shape=out_shape,
        in_specs=[ANY] * skipped + in_specs,
        out_specs=out_specs,
        scratch_shapes=scratch,
        cost_estimate=pl.CostEstimate(
            flops=int(micros * RATE), bytes_accessed=1000, transcendentals=0
        ),
        compiler_params=pltpu.CompilerParams(vmem_limit_bytes=room * 1024 * 1024),
        **extra,
    )
    return functools.partial(kernel, *earlier)


def lane_iota(shape):
    return lax.broadcasted_iota(jnp.int32, shape, len(shape) - 1)


def routing(ids, me, cap, experts):
    rows = ids.shape[1]
    expert = lax.broadcasted_iota(jnp.int32, (experts, rows), 0)
    onehot = jnp.where(expert == ids, 1.0, 0.0)
    before = lax.broadcasted_iota(jnp.int32, (rows, rows), 0) < lane_iota((rows, rows))
    earlier = jnp.dot(
        onehot.astype(BF16), jnp.where(before, 1.0, 0.0).astype(BF16), preferred_element_type=F32
    )
    rank = jnp.sum(earlier * onehot, axis=0, keepdims=True).astype(jnp.int32)
    slot = jnp.where(rank < cap, (ids ^ me) * cap + rank, experts * cap + rank - cap)
    slots = -(-(experts + 1) * cap // LANES) * LANES
    spread = lax.broadcasted_iota(jnp.int32, (slots, rows), 0) == slot
    return onehot, jnp.where(spread, 1.0, 0.0)


def softmax(logits):
    scores = jnp.exp(logits - jnp.max(logits, axis=0, keepdims=True))
    return scores / jnp.sum(scores, axis=0, keepdims=True)


def dispatch_body(plan, experts, cap, width, x_hbm, dy_hbm, logits_hbm, ids_hbm, *refs):
    outs, hot = refs[: len(plan)], refs[len(plan)]
    held, logits, ids, sems = refs[len(plan) + 1 :]
    loads = [
        pltpu.make_async_copy(ids_hbm, ids, sems.at[0]),
        pltpu.make_async_copy(logits_hbm, logits, sems.at[1]),
        pltpu.make_async_copy(x_hbm, held.at[0], sems.at[2]),
        pltpu.make_async_copy(dy_hbm, held.at[1], sems.at[3]),
    ]
    for load in loads:
        load.start()
    me = lax.axis_index("expert")
    slots = (experts + 1) * cap
    loads[0].wait()
    loads[1].wait()
    expert_ids = ids[...]
    onehot, spread = routing(expert_ids, me, cap, experts)
    spread = spread[:slots]
    gate = jnp.sum(softmax(logits[...]) * onehot, axis=0, keepdims=True)
    gate = gate.astype(BF16).astype(F32)
    mine = jnp.sum(jnp.where(expert_ids == me, 1, 0))
    hot[0] = jnp.where(mine > cap, 1, 0)
    counts = jnp.sum(onehot, axis=1, keepdims=True)
    expert = lax.broadcasted_iota(jnp.int32, (experts, LANES), 0)
    counts = jnp.sum(
        jnp.where(lane_iota((experts, LANES)) - COUNT_LANE == expert, counts, 0.0),
        axis=0,
        keepdims=True,
    )
    gates = jnp.sum(spread * gate, axis=1, keepdims=True)
    pad = jnp.where(lane_iota((slots, LANES)) == 0, gates, counts).astype(BF16)
    places = [(m, outs[i], j * cap) for i, held_by in enumerate(plan) for j, m in enumerate(held_by)]
    for m, out, first in places:
        out[first : first + cap, 2 * width :] = pad[m * cap : (m + 1) * cap]
    spread = spread.astype(BF16)
    tile = 1024
    for half in range(2):
        loads[2 + half].wait()
        for at in range(0, width, tile):
            moved = jnp.dot(
                spread, held[half, :, at : at + tile], preferred_element_type=F32
            ).astype(BF16)
            for m, out, first in places:
                out[first : first + cap, half * width + at : half * width + at + tile] = moved[
                    m * cap : (m + 1) * cap
                ]


def dispatch(rows_x, rows_dy, logits, ids, experts, cap, plan):
    rows, width = rows_x.shape
    wide = 2 * width + LANES
    return call(
        functools.partial(dispatch_body, plan, experts, cap, width),
        "dispatch",
        [jax.ShapeDtypeStruct((len(held_by) * cap, wide), BF16) for held_by in plan]
        + [jax.ShapeDtypeStruct((1,), jnp.int32)],
        [HBM] * 4,
        [VMEM] * len(plan) + [SMEM],
        [
            pltpu.VMEM((2, rows, width), BF16),
            pltpu.VMEM(logits.shape, F32),
            pltpu.VMEM(ids.shape, jnp.int32),
            pltpu.SemaphoreType.DMA((4,)),
        ],
        6,
        58,
    )(rows_x, rows_dy, logits, ids)


def split_lanes(total):
    lane = lane_iota((total.shape[0], LANES))
    first = total.astype(BF16).astype(F32)
    second = (total - first).astype(BF16).astype(F32)
    third = total - first - second
    return jnp.where(
        lane == 0, first, jnp.where(lane == 1, second, jnp.where(lane == 2, third, 0.0))
    ).astype(BF16)


def rows_body(ranges, width, n_dp, guarded, hot, *refs):
    pieces = len(ranges)
    sources, weights = refs[:pieces], refs[pieces : pieces + 3]
    outs = refs[pieces + 3 : -2]
    held, piece_sems = refs[-2:]
    hidden_units = weights[0].shape[0]
    rows = held.shape[0]

    def work():
        copies, at = [], 0
        for p in range(pieces):
            first, count = ranges[p]
            copies.append(
                pltpu.make_async_copy(
                    sources[p].at[pl.ds(first, count), :],
                    held.at[pl.ds(at, count), :],
                    piece_sems.at[p],
                )
            )
            at += count
        for copy in copies:
            copy.start()
        for copy in copies:
            copy.wait()
        pre_gate, pre_up, grad = [
            lax.dot_general(
                held[:, side * width : (side + 1) * width],
                weight[...],
                (((1,), (1,)), ((), ())),
                preferred_element_type=F32,
            )
            for side, weight in zip((0, 0, 1), weights)
        ]
        gate = held[:, 2 * width :].astype(F32)[:, 0:1]
        sigmoid = jax.nn.sigmoid(pre_gate)
        active = pre_gate * sigmoid
        hidden = (active * pre_up).astype(BF16)
        hidden_f = hidden.astype(F32)
        gate_part = jnp.sum(hidden_f * grad, axis=1, keepdims=True)
        grad_hidden = grad * gate
        d_up = (grad_hidden * active).astype(BF16)
        d_pre = (grad_hidden * pre_up * sigmoid * (1.0 + pre_gate * (1.0 - sigmoid))).astype(BF16)
        outs[-1][:, :hidden_units] = d_pre
        outs[-1][:, hidden_units : 2 * hidden_units] = d_up
        outs[-1][:, 2 * hidden_units :] = (hidden_f * gate).astype(BF16)
        lanes = split_lanes(gate_part)
        cut = width // n_dp
        part = n_dp // 2 * cut + LANES
        me = lax.axis_index("dp")
        for half in range(2):
            places = [(outs[half], 0)]
            if guarded:
                places.append((outs[2 + half], rows // 2))
            for out, first in places:
                count = out.shape[0]
                out[:, part - LANES :] = lanes[first : first + count]
                for p in range(n_dp // 2):
                    column = pl.multiple_of((me ^ (2 * p + half)) * cut, cut)
                    out[:, p * cut : (p + 1) * cut] = (
                        jnp.dot(
                            d_pre[first : first + count],
                            weights[0][:, pl.ds(column, cut)],
                            preferred_element_type=F32,
                        )
                        + jnp.dot(
                            d_up[first : first + count],
                            weights[1][:, pl.ds(column, cut)],
                            preferred_element_type=F32,
                        )
                    ).astype(BF16)

    if guarded:

        @pl.when(hot[0] == 1)
        def _():
            work()

        @pl.when(hot[0] != 1)
        def _():
            for out in outs:
                out[...] = jnp.zeros_like(out)
    else:
        work()


def rows_backward(earlier, hot, parts, weights, n_dp, guarded, micros=0.001):
    width = weights[0].shape[1]
    hidden_units = weights[0].shape[0]
    sources = [source for source, _, _ in parts]
    ranges = [(first, count) for _, first, count in parts]
    rows = sum(count for _, count in ranges)
    part = width // 2 + LANES
    shapes = [(rows // 2, part)] * 4 if guarded else [(rows, part)] * 2
    return call(
        functools.partial(rows_body, ranges, width, n_dp, guarded),
        "rows_backward",
        [jax.ShapeDtypeStruct(s, BF16) for s in shapes]
        + [jax.ShapeDtypeStruct((rows, 3 * hidden_units), BF16)],
        [SMEM] + [ANY] * len(sources) + [VMEM] * 3,
        [VMEM] * (len(shapes) + 1),
        [
            pltpu.VMEM((rows, 2 * width + LANES), BF16),
            pltpu.SemaphoreType.DMA((len(sources),)),
        ],
        micros,
        20,
        earlier,
    )(hot, *sources, *weights)


def merge_body(own, peers, out):
    out[...] = own[...] + peers[...]


def merge(earlier, own, peers):
    return call(
        merge_body,
        "merge",
        [jax.ShapeDtypeStruct(own.shape, BF16)],
        [VMEM] * 2,
        [VMEM],
        [],
        0.001,
        8,
        earlier,
    )(own, peers)


def sum_of(parts, columns):
    return functools.reduce(jnp.add, [part[:, columns].astype(F32) for part in parts])


def fold_body(cut, parts, count, *refs):
    given, outs = refs[:count], refs[count:]
    total = sum_of(given, slice(parts * cut, None))
    lanes = split_lanes(jnp.sum(total, axis=1, keepdims=True))
    for out in outs:
        out[:, parts // 2 * cut :] = lanes
    for p in range(parts):
        columns = slice(p * cut, (p + 1) * cut)
        outs[p % 2][:, p // 2 * cut : (p // 2 + 1) * cut] = sum_of(given, columns).astype(BF16)


def fold(earlier, given, cut):
    rows = given[0].shape[0]
    parts = (given[0].shape[1] - LANES) // cut
    shape = jax.ShapeDtypeStruct((rows, parts // 2 * cut + LANES), BF16)
    return call(
        functools.partial(fold_body, cut, parts, len(given)),
        "fold",
        [shape] * 2,
        [VMEM] * len(given),
        [VMEM] * 2,
        [],
        0.001,
        8,
        earlier,
    )(*given)


def tree(values):
    while len(values) > 1:
        values = [a + b for a, b in zip(values[::2], values[1::2])]
    return values[0]


def last_body(cut, cap, places, count, *refs):
    pairs = len(places)
    squares, given, outs = refs[:count], refs[count : count + 2 * pairs], refs[count + 2 * pairs :]
    total = tree([part[0:1, 0:1] for part in squares])
    lane = lane_iota((1, LANES))
    square = jnp.zeros((1, LANES), F32)
    for i in range(3):
        part = total.astype(BF16).astype(F32)
        square = jnp.where(lane == SQUARE_LANE + i, part, square)
        total = total - part
    for i, where in enumerate(places):
        pair = given[2 * i : 2 * i + 2]
        whole = sum_of(pair, slice(0, cut)).astype(BF16)
        gates = jnp.sum(sum_of(pair, slice(cut, None)), axis=1, keepdims=True)
        lanes = jnp.where(lane == 0, gates, square).astype(BF16)
        for start, out, first in where:
            outs[out][first : first + cap, :cut] = whole[start : start + cap]
            outs[out][first : first + cap, cut:] = lanes[start : start + cap]


def last(earlier, squares, pairs, chunks, masks, cut, cap):
    places = []
    for i, chunk in enumerate(chunks):
        first = cap if i == len(chunks) - 1 else 0
        places.append([(j * cap, masks.index(m), first) for j, m in enumerate(chunk) if m in masks])
    return call(
        functools.partial(last_body, cut, cap, places, len(squares)),
        "last",
        [jax.ShapeDtypeStruct((cap if m % 2 else 2 * cap, cut + LANES), BF16) for m in masks],
        [VMEM] * (len(squares) + 2 * len(pairs)),
        [VMEM] * len(masks),
        [],
        0.001,
        12,
        earlier,
    )(*squares, *[part for pair in pairs for part in pair])


def weights_body(ranges, cold_pieces, acts_count, width, tile, hot, *refs):
    pieces = len(ranges)
    sources, acts = refs[:pieces], refs[pieces : pieces + acts_count]
    outs, squares = refs[pieces + acts_count : -4][:3], refs[pieces + acts_count : -4][3]
    held, factors, total, sems = refs[-4:]
    step = pl.program_id(0)
    hidden_units = outs[0].shape[0]

    starts = [sum(count for _, count in ranges[:p]) for p in range(pieces + 1)]

    def copies(count):
        return [
            pltpu.make_async_copy(
                sources[p].at[pl.ds(ranges[p][0], ranges[p][1]), pl.ds(0, 2 * width)],
                held.at[pl.ds(starts[p], ranges[p][1]), :],
                sems.at[p],
            )
            for p in count
        ]

    @pl.when(step == 0)
    def _():
        for copy in copies(range(cold_pieces)):
            copy.start()

        @pl.when(hot[0] == 1)
        def _():
            for copy in copies(range(cold_pieces, pieces)):
                copy.start()

        at = 0
        for act in acts:
            factors[:, at : at + act.shape[0]] = act[...].astype(F32).T.astype(BF16)
            at += act.shape[0]
        total[...] = jnp.zeros_like(total)
        for copy in copies(range(cold_pieces)):
            copy.wait()

        @pl.when(hot[0] == 1)
        def _():
            for copy in copies(range(cold_pieces, pieces)):
                copy.wait()

    def work(rows):
        for i in range(3):
            at = pl.multiple_of((width if i == 2 else 0) + step * tile, tile)
            gradient = jnp.dot(
                factors[i * hidden_units : (i + 1) * hidden_units, :rows],
                held[:rows, pl.ds(at, tile)],
                preferred_element_type=F32,
            )
            outs[i][...] = gradient
            total[...] += jnp.sum((gradient * gradient).reshape(-1, 8, tile), axis=0)

    @pl.when(hot[0] == 1)
    def _():
        work(starts[pieces])

    @pl.when(hot[0] != 1)
    def _():
        work(starts[cold_pieces])

    @pl.when(step == pl.num_programs(0) - 1)
    def _():
        squares[...] = jnp.full(squares.shape, jnp.sum(total[...]), F32)


def weights_backward(earlier, hot, cold, extra, acts, hidden_units, width):
    tile = 512
    sources = [source for source, _, _ in cold + extra]
    ranges = [(first, count) for _, first, count in cold + extra]
    rows = sum(count for _, count in ranges)
    block = pl.BlockSpec((hidden_units, tile), lambda j: (0, j))
    whole = [pl.BlockSpec(a.shape, lambda j: (0, 0)) for a in acts]
    return call(
        functools.partial(
            weights_body, ranges, len(cold), len(acts), width, tile
        ),
        "weights_backward",
        [jax.ShapeDtypeStruct((hidden_units, width), F32)] * 3
        + [jax.ShapeDtypeStruct((8, LANES), F32)],
        [SMEM] + [ANY] * len(sources) + whole,
        [block] * 3 + [pl.BlockSpec((8, LANES), lambda j: (0, 0))],
        [
            pltpu.VMEM((rows, 2 * width), BF16),
            pltpu.VMEM((3 * hidden_units, rows), BF16),
            pltpu.VMEM((8, tile), F32),
            pltpu.SemaphoreType.DMA((len(sources),)),
        ],
        0.001,
        24,
        earlier,
        grid=(width // tile,),
    )(hot, *sources, *acts)


def home_body(experts, cap, cut, row_total, firsts, logits, ids, *refs):
    arrived, back = refs[:experts], refs[experts : 2 * experts]
    grad_rows, grad_logits, norm, pads, table, sems = refs[2 * experts :]
    copies = [
        pltpu.make_async_copy(
            arrived[m].at[pl.ds(firsts[m], 16), pl.ds(arrived[m].shape[1] - LANES, LANES)],
            pads.at[pl.ds(16 * m, 16), :],
            sems.at[m],
        )
        for m in range(experts)
    ]
    for copy in copies:
        copy.start()
    onehot, spread = routing(ids[...], lax.axis_index("expert"), cap, experts)
    slots = (experts + 1) * cap
    for m in range(experts):
        table[m * cap : (m + 1) * cap, :] = back[m][:cap, :]
    over = back[0][cap:, :]
    for m in range(2, experts, 2):
        over = over + back[m][cap:, :]
    table[experts * cap :, :] = over
    lane = lane_iota((8, LANES))
    square = tree([back[m][0:16, cut:].astype(F32)[0:8] for m in range(experts)])
    square = jnp.where((lane >= SQUARE_LANE) & (lane < SQUARE_LANE + 3), square, 0.0)
    norm[0] = jnp.max(jnp.sqrt(jnp.sum(square, axis=1, keepdims=True)))
    pick = spread.T[:, :slots].astype(BF16)
    grad_rows[...] = jnp.dot(pick, table[:, :cut], preferred_element_type=F32).astype(BF16)
    gate_rows = jnp.dot(pick, table[:, cut:], preferred_element_type=F32).T[0:1]
    for copy in copies:
        copy.wait()
    counts = jnp.zeros((1, LANES), F32)
    for m in range(experts):
        counts = counts + pads[16 * m : 16 * m + 16, :].astype(F32)[0:1]
    counts = jnp.broadcast_to(counts, (8, LANES)).T[COUNT_LANE : COUNT_LANE + experts, 0:1]
    probs = softmax(logits[...])
    pulls = onehot * gate_rows + aux_weight * experts * (counts / row_total)
    grad_logits[...] = probs * (pulls - jnp.sum(probs * pulls, axis=0, keepdims=True))


def home(logits, ids, arrived, back, cap, row_total):
    experts = len(back)
    rows = ids.shape[1]
    cut = back[0].shape[1] - LANES
    return call(
        functools.partial(
            home_body, experts, cap, cut, row_total, [first for _, first, _ in arrived]
        ),
        "home",
        [
            jax.ShapeDtypeStruct((rows, cut), BF16),
            jax.ShapeDtypeStruct(logits.shape, F32),
            jax.ShapeDtypeStruct((1,), F32),
        ],
        [VMEM, VMEM] + [ANY] * experts + [VMEM] * experts,
        [VMEM, VMEM, SMEM],
        [
            pltpu.VMEM((16 * experts, LANES), BF16),
            pltpu.VMEM(((experts + 1) * cap, cut + LANES), BF16),
            pltpu.SemaphoreType.DMA((experts,)),
        ],
        0.001,
        12,
    )(logits, ids, *[piece for piece, _, _ in arrived], *back)


def swap(value, axis, mask):
    size = lax.axis_size(axis)
    return lax.ppermute(value, axis, [(i, i ^ mask) for i in range(size)])


def after(values, done):
    tied = lax.optimization_barrier((*values, *done))
    return tied[: len(values)], tied[len(values) :]


def local(rows_x, rows_dy, router_logits, expert_of, w_gate, w_up, w_down):
    experts = lax.axis_size("expert")
    n_dp = lax.axis_size("dp")
    rows, width = rows_x.shape
    cap = rows // 8
    cut = width // n_dp
    weights = (w_gate[0], w_up[0], w_down[0])
    hidden_units = weights[0].shape[0]
    logits, ids = router_logits.T, expert_of.reshape(1, rows)
    evens = list(range(0, experts, 2))
    near = [m for m in evens[1:] if m & (m - 1) == 0]
    far = [m for m in evens[1:] if m & (m - 1)]
    path = {m: [b for b in near if m & b] for m in far}
    path.update({m ^ 1: [b for b in near[::-1] if m & b] for m in far})
    first_hop = {b: [m for m in path if path[m][0] == b] for b in near}
    plan = [[0], [1, experts, *range(3, experts, 2)], [experts]]
    plan += [[b] + [m for m in first_hop[b] if m % 2 == 0] for b in near]
    own, beside, spare, *mine, hot = dispatch(
        rows_x, rows_dy, logits, ids, experts, cap, plan
    )
    bits = [1 << i for i in range(n_dp.bit_length() - 1)]
    token = []

    def step(kernel, *given):
        result = kernel(tuple(token), *given)
        token[:] = [result[-1]]
        return result

    def wait_for(*arrived):
        token.extend(arrived)

    def backward(parts, kind=False, micros=0.001):
        return step(rows_backward, hot, parts, weights, n_dp, kind, micros)

    def turn(pair, bit):
        *kept, sent = pair
        return *kept, swap(sent, "dp", bit)

    def middle(pair):
        for bit in bits[1:]:
            pair = turn(step(fold, pair, cut), bit)
        return pair

    beside = swap(beside, "expert", 1)

    def from_beside(m):
        at = plan[1].index(m) * cap
        return beside[at : at + cap]

    cold = {0: (own, 0, cap), 1: (beside, 0, cap)}
    chunks = [[0, 1], [m ^ c for c in (0, 1) for m in near], [m ^ c for c in (0, 1) for m in far]]
    over = {m: swap(spare, "expert", m) for m in near}
    *first, acts_first = backward([cold[m] for m in chunks[0]])
    (later,), (acts_first,) = after([spare], [acts_first])
    over.update({m: swap(later, "expert", m) for m in far})
    over = [over[m] for m in evens[1:]]
    kept, sent = step(fold, turn(first, bits[0]), cut)
    packed, (sent,) = after(over, [sent])
    crossed = swap(jnp.concatenate(packed, axis=0), "expert", 1)
    first = turn((kept, sent), bits[1])
    for bit in bits[2:]:
        first = turn(step(fold, first, cut), bit)
    loads = []
    for b, part in zip(near, mine):
        odd = [b ^ 1] + [m for m in first_hop[b] if m % 2]
        loads.append(jnp.concatenate([part] + [from_beside(m) for m in odd], axis=0))
    loads, over = after(loads, over)
    extras = [(part, 0, cap) for part in [spare, *over]]
    extras += [(beside, cap, cap), (crossed, 0, crossed.shape[0])]
    loads = [swap(load, "expert", b) for b, load in zip(near, loads)]

    kept, sent, far_kept, far_sent, acts_hot = backward(extras, True)
    far_sent = swap(far_sent, "expert", 1)
    far_kept = swap(far_kept, "expert", 1)
    (sent,) = step(merge, sent, far_sent)
    wait_for(first[-1])
    busy = turn((kept, far_kept, sent), bits[0])
    busy = middle(busy)
    passed = {}
    for b, load in zip(near, loads):
        items = [b] + [m for m in first_hop[b] if m % 2 == 0]
        items += [b ^ 1] + [m for m in first_hop[b] if m % 2]
        for i, m in enumerate(items):
            if m in path:
                passed[m] = load[i * cap : (i + 1) * cap]
            else:
                cold[m] = (load, i * cap, cap)
    on_way = list(passed)
    parts, (met,) = after([passed[m] for m in on_way], [busy[-1]])
    busy = (*busy[:-1], met)
    for m, part in zip(on_way, parts):
        for b in path[m][1:]:
            part = swap(part, "expert", b)
        cold[m] = (part, 0, cap)
    *second, acts_second = backward([cold[m] for m in chunks[1]])
    second = turn(second, bits[0])
    *third, acts_third = backward([cold[m] for m in chunks[2]])
    third = turn(third, bits[0])
    second = middle(second)
    grad_gate, grad_up, grad_down, squares = step(
        weights_backward,
        hot,
        [cold[m] for m in sum(chunks, [])],
        extras,
        [acts_first, acts_second, acts_third, acts_hot],
        hidden_units,
        width,
    )
    for bit in bits[1:]:
        kept, sent = step(fold, third, cut)
        (squares,), (sent,) = after([squares], [sent])
        third = turn((kept, sent), bit)
    squares = [squares] + [swap(squares, "dp", m) for m in range(1, n_dp)]
    back = {}
    for masks, pairs, where in (
        (chunks[0] + chunks[1], [first, second, busy], [*chunks[:2], evens]),
        (chunks[2], [third, busy], [chunks[2], evens]),
    ):
        for m, piece in zip(masks, step(last, squares, pairs, where, masks, cut, cap)):
            back[m] = piece if m == 0 else swap(piece, "expert", m)
    grad_rows, grad_logits, norm = home(
        logits,
        ids,
        [cold[m] for m in range(experts)],
        [back[m] for m in range(experts)],
        cap,
        rows * experts,
    )
    return (
        grad_rows,
        grad_logits.T,
        grad_gate[None],
        grad_up[None],
        grad_down[None],
        norm.reshape(()),
    )


def solution(mesh):
    in_specs = (
        P("expert", None),
        P("expert", None),
        P("expert", None),
        P("expert", None),
        P("expert", "dp", None),
        P("expert", "dp", None),
        P("expert", "dp", None),
    )
    out_specs = (
        P("expert", "dp"),
        P("expert", None),
        P("expert", "dp", None),
        P("expert", "dp", None),
        P("expert", "dp", None),
        P(),
    )
    return jax.shard_map(local, mesh=mesh, in_specs=in_specs, out_specs=out_specs, check_vma=False)
```

```python
import functools

import jax
import jax.numpy as jnp
from jax import lax
from jax.experimental import pallas as pl
from jax.experimental.pallas import tpu as pltpu
from jax.sharding import PartitionSpec as P

aux_weight = 1.0
LANES = 128
COUNT_LANE = 64
RATE = 1e9
SQUARE_LANE = 8
BF16 = jnp.bfloat16
F32 = jnp.float32
ANY = pl.BlockSpec(memory_space=pl.ANY)
VMEM = pl.BlockSpec(memory_space=pltpu.VMEM)
SMEM = pl.BlockSpec(memory_space=pltpu.SMEM)
HBM = pl.BlockSpec(memory_space=pltpu.HBM)


def call(body, name, out_shape, in_specs, out_specs, scratch, micros, room, earlier=(), **extra):
    skipped = len(earlier)

    def without(*refs):
        body(*refs[skipped:])

    kernel = pl.pallas_call(
        without,
        name=name,
        out_shape=out_shape,
        in_specs=[ANY] * skipped + in_specs,
        out_specs=out_specs,
        scratch_shapes=scratch,
        cost_estimate=pl.CostEstimate(
            flops=int(micros * RATE), bytes_accessed=1000, transcendentals=0
        ),
        compiler_params=pltpu.CompilerParams(vmem_limit_bytes=room * 1024 * 1024),
        **extra,
    )
    return functools.partial(kernel, *earlier)


def lane_iota(shape):
    return lax.broadcasted_iota(jnp.int32, shape, len(shape) - 1)


def routing(ids, me, cap, experts):
    rows = ids.shape[1]
    expert = lax.broadcasted_iota(jnp.int32, (experts, rows), 0)
    onehot = jnp.where(expert == ids, 1.0, 0.0)
    before = lax.broadcasted_iota(jnp.int32, (rows, rows), 0) < lane_iota((rows, rows))
    earlier = jnp.dot(
        onehot.astype(BF16), jnp.where(before, 1.0, 0.0).astype(BF16), preferred_element_type=F32
    )
    rank = jnp.sum(earlier * onehot, axis=0, keepdims=True).astype(jnp.int32)
    slot = jnp.where(rank < cap, (ids ^ me) * cap + rank, experts * cap + rank - cap)
    slots = -(-(experts + 1) * cap // LANES) * LANES
    spread = lax.broadcasted_iota(jnp.int32, (slots, rows), 0) == slot
    return onehot, jnp.where(spread, 1.0, 0.0)


def softmax(logits):
    scores = jnp.exp(logits - jnp.max(logits, axis=0, keepdims=True))
    return scores / jnp.sum(scores, axis=0, keepdims=True)


def dispatch_body(plan, experts, cap, width, x_hbm, dy_hbm, logits_hbm, ids_hbm, *refs):
    outs, part, hot = refs[: len(plan)], refs[len(plan)], refs[len(plan) + 1]
    held, logits, ids, sems = refs[len(plan) + 2 :]
    loads = [
        pltpu.make_async_copy(ids_hbm, ids, sems.at[0]),
        pltpu.make_async_copy(logits_hbm, logits, sems.at[1]),
        pltpu.make_async_copy(x_hbm, held.at[0], sems.at[2]),
        pltpu.make_async_copy(dy_hbm, held.at[1], sems.at[3]),
    ]
    for load in loads:
        load.start()
    me = lax.axis_index("expert")
    slots = (experts + 1) * cap
    loads[0].wait()
    loads[1].wait()
    expert_ids = ids[...]
    onehot, spread = routing(expert_ids, me, cap, experts)
    spread = spread[:slots]
    gate = jnp.sum(softmax(logits[...]) * onehot, axis=0, keepdims=True)
    gate = gate.astype(BF16).astype(F32)
    mine = jnp.sum(jnp.where(expert_ids == me, 1, 0))
    hot[0] = jnp.where(mine > cap, 1, 0)
    counts = jnp.sum(onehot, axis=1, keepdims=True)
    expert = lax.broadcasted_iota(jnp.int32, (experts, LANES), 0)
    counts = jnp.sum(
        jnp.where(lane_iota((experts, LANES)) - COUNT_LANE == expert, counts, 0.0),
        axis=0,
        keepdims=True,
    )
    gates = jnp.sum(spread * gate, axis=1, keepdims=True)
    pad = jnp.where(lane_iota((slots, LANES)) == 0, gates, counts).astype(BF16)
    places = [(m, outs[i], j * cap) for i, held_by in enumerate(plan) for j, m in enumerate(held_by)]
    for m, out, first in places:
        out[first : first + cap, 2 * width :] = pad[m * cap : (m + 1) * cap]
    part[:, width:] = pad[experts * cap :]
    parity = lax.rem(lax.axis_index("dp"), 2)
    spread = spread.astype(BF16)
    tile = 1024
    for half in range(2):
        loads[2 + half].wait()
        for at in range(0, width, tile):
            moved = jnp.dot(
                spread, held[half, :, at : at + tile], preferred_element_type=F32
            ).astype(BF16)
            for m, out, first in places:
                out[first : first + cap, half * width + at : half * width + at + tile] = moved[
                    m * cap : (m + 1) * cap
                ]

            @pl.when(parity == half)
            def _():
                part[:, at : at + tile] = moved[experts * cap :]


def dispatch(rows_x, rows_dy, logits, ids, experts, cap, plan):
    rows, width = rows_x.shape
    wide = 2 * width + LANES
    return call(
        functools.partial(dispatch_body, plan, experts, cap, width),
        "dispatch",
        [jax.ShapeDtypeStruct((len(held_by) * cap, wide), BF16) for held_by in plan]
        + [jax.ShapeDtypeStruct((cap, width + LANES), BF16)]
        + [jax.ShapeDtypeStruct((1,), jnp.int32)],
        [HBM] * 4,
        [VMEM] * (len(plan) + 1) + [SMEM],
        [
            pltpu.VMEM((2, rows, width), BF16),
            pltpu.VMEM(logits.shape, F32),
            pltpu.VMEM(ids.shape, jnp.int32),
            pltpu.SemaphoreType.DMA((4,)),
        ],
        6,
        58,
    )(rows_x, rows_dy, logits, ids)


def split_lanes(total):
    lane = lane_iota((total.shape[0], LANES))
    first = total.astype(BF16).astype(F32)
    second = (total - first).astype(BF16).astype(F32)
    third = total - first - second
    return jnp.where(
        lane == 0, first, jnp.where(lane == 1, second, jnp.where(lane == 2, third, 0.0))
    ).astype(BF16)


def moves(ranges, width, extra):
    parity = lax.rem(lax.axis_index("dp"), 2)
    found, at = [], 0
    for p, (first, count, side) in enumerate(ranges):
        if side is None:
            found.append((p, first, count, 0, 2 * width + extra, at, 0))
        elif side == "this":
            found.append((p, first, count, 0, width, at, pl.multiple_of(parity * width, width)))
            if extra:
                found.append((p, first, count, width, extra, at, 2 * width))
        else:
            at -= count
            column = pl.multiple_of((1 - parity) * width, width)
            found.append((p, first, count, 0, width, at, column))
        at += count
    return found


def rows_in(ranges):
    return sum(count for _, count, side in ranges if side != "that")


def rows_body(ranges, width, n_dp, guarded, hot, *refs):
    pieces = len(ranges)
    sources, weights = refs[:pieces], refs[pieces : pieces + 3]
    outs = refs[pieces + 3 : -2]
    held, piece_sems = refs[-2:]
    hidden_units = weights[0].shape[0]
    rows = held.shape[0]

    def work():
        copies = [
            pltpu.make_async_copy(
                sources[p].at[pl.ds(first, count), pl.ds(column, columns)],
                held.at[pl.ds(at, count), pl.ds(target, columns)],
                piece_sems.at[i],
            )
            for i, (p, first, count, column, columns, at, target) in enumerate(
                moves(ranges, width, LANES)
            )
        ]
        for copy in copies:
            copy.start()
        for copy in copies:
            copy.wait()
        pre_gate, pre_up, grad = [
            lax.dot_general(
                held[:, side * width : (side + 1) * width],
                weight[...],
                (((1,), (1,)), ((), ())),
                preferred_element_type=F32,
            )
            for side, weight in zip((0, 0, 1), weights)
        ]
        gate = held[:, 2 * width :].astype(F32)[:, 0:1]
        sigmoid = jax.nn.sigmoid(pre_gate)
        active = pre_gate * sigmoid
        hidden = (active * pre_up).astype(BF16)
        hidden_f = hidden.astype(F32)
        gate_part = jnp.sum(hidden_f * grad, axis=1, keepdims=True)
        grad_hidden = grad * gate
        d_up = (grad_hidden * active).astype(BF16)
        d_pre = (grad_hidden * pre_up * sigmoid * (1.0 + pre_gate * (1.0 - sigmoid))).astype(BF16)
        outs[-1][:, :hidden_units] = d_pre
        outs[-1][:, hidden_units : 2 * hidden_units] = d_up
        outs[-1][:, 2 * hidden_units :] = (hidden_f * gate).astype(BF16)
        lanes = split_lanes(gate_part)
        cut = width // n_dp
        part = n_dp // 2 * cut + LANES
        me = lax.axis_index("dp")
        for half in range(2):
            places = [(outs[half], 0)]
            if guarded:
                places.append((outs[2 + half], rows // 2))
            for out, first in places:
                count = out.shape[0]
                out[:, part - LANES :] = lanes[first : first + count]
                for p in range(n_dp // 2):
                    column = pl.multiple_of((me ^ (2 * p + half)) * cut, cut)
                    out[:, p * cut : (p + 1) * cut] = (
                        jnp.dot(
                            d_pre[first : first + count],
                            weights[0][:, pl.ds(column, cut)],
                            preferred_element_type=F32,
                        )
                        + jnp.dot(
                            d_up[first : first + count],
                            weights[1][:, pl.ds(column, cut)],
                            preferred_element_type=F32,
                        )
                    ).astype(BF16)

    if guarded:

        @pl.when(hot[0] == 1)
        def _():
            work()

        @pl.when(hot[0] != 1)
        def _():
            for out in outs:
                out[...] = jnp.zeros_like(out)
    else:
        work()


def rows_backward(earlier, hot, parts, weights, n_dp, guarded, micros=0.001):
    width = weights[0].shape[1]
    hidden_units = weights[0].shape[0]
    sources = [source for source, *_ in parts]
    ranges = [tuple(where) for _, *where in parts]
    rows = rows_in(ranges)
    part = width // 2 + LANES
    shapes = [(rows // 2, part)] * 4 if guarded else [(rows, part)] * 2
    return call(
        functools.partial(rows_body, ranges, width, n_dp, guarded),
        "rows_backward",
        [jax.ShapeDtypeStruct(s, BF16) for s in shapes]
        + [jax.ShapeDtypeStruct((rows, 3 * hidden_units), BF16)],
        [SMEM] + [ANY] * len(sources) + [VMEM] * 3,
        [VMEM] * (len(shapes) + 1),
        [
            pltpu.VMEM((rows, 2 * width + LANES), BF16),
            pltpu.SemaphoreType.DMA((2 * len(sources),)),
        ],
        micros,
        20,
        earlier,
    )(hot, *sources, *weights)


def merge_body(own, peers, out):
    out[...] = own[...] + peers[...]


def merge(earlier, own, peers):
    return call(
        merge_body,
        "merge",
        [jax.ShapeDtypeStruct(own.shape, BF16)],
        [VMEM] * 2,
        [VMEM],
        [],
        0.001,
        8,
        earlier,
    )(own, peers)


def sum_of(parts, columns):
    return functools.reduce(jnp.add, [part[:, columns].astype(F32) for part in parts])


def fold_body(cut, parts, count, *refs):
    given, outs = refs[:count], refs[count:]
    total = sum_of(given, slice(parts * cut, None))
    lanes = split_lanes(jnp.sum(total, axis=1, keepdims=True))
    for out in outs:
        out[:, parts // 2 * cut :] = lanes
    for p in range(parts):
        columns = slice(p * cut, (p + 1) * cut)
        outs[p % 2][:, p // 2 * cut : (p // 2 + 1) * cut] = sum_of(given, columns).astype(BF16)


def fold(earlier, given, cut):
    rows = given[0].shape[0]
    parts = (given[0].shape[1] - LANES) // cut
    shape = jax.ShapeDtypeStruct((rows, parts // 2 * cut + LANES), BF16)
    return call(
        functools.partial(fold_body, cut, parts, len(given)),
        "fold",
        [shape] * 2,
        [VMEM] * len(given),
        [VMEM] * 2,
        [],
        0.001,
        8,
        earlier,
    )(*given)


def tree(values):
    while len(values) > 1:
        values = [a + b for a, b in zip(values[::2], values[1::2])]
    return values[0]


def last_body(cut, cap, places, count, *refs):
    pairs = len(places)
    squares, given, outs = refs[:count], refs[count : count + 2 * pairs], refs[count + 2 * pairs :]
    total = tree([part[0:1, 0:1] for part in squares]) if squares else jnp.zeros((1, 1), F32)
    lane = lane_iota((1, LANES))
    square = jnp.zeros((1, LANES), F32)
    for i in range(3):
        part = total.astype(BF16).astype(F32)
        square = jnp.where(lane == SQUARE_LANE + i, part, square)
        total = total - part
    for i, where in enumerate(places):
        pair = given[2 * i : 2 * i + 2]
        whole = sum_of(pair, slice(0, cut)).astype(BF16)
        gates = jnp.sum(sum_of(pair, slice(cut, None)), axis=1, keepdims=True)
        lanes = jnp.where(lane == 0, gates, square).astype(BF16)
        for start, out in where:
            outs[out][:, :cut] = whole[start : start + cap]
            outs[out][:, cut:] = lanes[start : start + cap]


def last(earlier, squares, pairs, chunks, masks, cut, cap):
    places = [[(j * cap, masks.index(m)) for j, m in enumerate(chunk)] for chunk in chunks]
    return call(
        functools.partial(last_body, cut, cap, places, len(squares)),
        "last",
        [jax.ShapeDtypeStruct((cap, cut + LANES), BF16)] * len(masks),
        [VMEM] * (len(squares) + 2 * len(pairs)),
        [VMEM] * len(masks),
        [],
        0.001,
        12,
        earlier,
    )(*squares, *[part for pair in pairs for part in pair])


def weights_body(ranges, cold_pieces, acts_count, width, tile, hot, *refs):
    pieces = len(ranges)
    sources, acts = refs[:pieces], refs[pieces : pieces + acts_count]
    outs, squares = refs[pieces + acts_count : -4][:3], refs[pieces + acts_count : -4][3]
    held, factors, total, sems = refs[-4:]
    step = pl.program_id(0)
    hidden_units = outs[0].shape[0]


    def copies(count):
        return [
            pltpu.make_async_copy(
                sources[p].at[pl.ds(first, size), pl.ds(column, columns)],
                held.at[pl.ds(at, size), pl.ds(target, columns)],
                sems.at[p],
            )
            for p, first, size, column, columns, at, target in moves(ranges, width, 0)
            if p in count
        ]

    @pl.when(step == 0)
    def _():
        for copy in copies(range(cold_pieces)):
            copy.start()

        @pl.when(hot[0] == 1)
        def _():
            for copy in copies(range(cold_pieces, pieces)):
                copy.start()

        at = 0
        for act in acts:
            factors[:, at : at + act.shape[0]] = act[...].astype(F32).T.astype(BF16)
            at += act.shape[0]
        total[...] = jnp.zeros_like(total)
        for copy in copies(range(cold_pieces)):
            copy.wait()

        @pl.when(hot[0] == 1)
        def _():
            for copy in copies(range(cold_pieces, pieces)):
                copy.wait()

    def work(rows):
        for i in range(3):
            at = pl.multiple_of((width if i == 2 else 0) + step * tile, tile)
            gradient = jnp.dot(
                factors[i * hidden_units : (i + 1) * hidden_units, :rows],
                held[:rows, pl.ds(at, tile)],
                preferred_element_type=F32,
            )
            outs[i][...] = gradient
            total[...] += jnp.sum((gradient * gradient).reshape(-1, 8, tile), axis=0)

    @pl.when(hot[0] == 1)
    def _():
        work(rows_in(ranges))

    @pl.when(hot[0] != 1)
    def _():
        work(rows_in(ranges[:cold_pieces]))

    @pl.when(step == pl.num_programs(0) - 1)
    def _():
        squares[...] = jnp.full(squares.shape, jnp.sum(total[...]), F32)


def weights_backward(earlier, hot, cold, extra, acts, hidden_units, width):
    tile = 512
    sources = [source for source, *_ in cold + extra]
    ranges = [tuple(where) for _, *where in cold + extra]
    rows = rows_in(ranges)
    block = pl.BlockSpec((hidden_units, tile), lambda j: (0, j))
    whole = [pl.BlockSpec(a.shape, lambda j: (0, 0)) for a in acts]
    return call(
        functools.partial(
            weights_body, ranges, len(cold), len(acts), width, tile
        ),
        "weights_backward",
        [jax.ShapeDtypeStruct((hidden_units, width), F32)] * 3
        + [jax.ShapeDtypeStruct((8, LANES), F32)],
        [SMEM] + [ANY] * len(sources) + whole,
        [block] * 3 + [pl.BlockSpec((8, LANES), lambda j: (0, 0))],
        [
            pltpu.VMEM((rows, 2 * width), BF16),
            pltpu.VMEM((3 * hidden_units, rows), BF16),
            pltpu.VMEM((8, tile), F32),
            pltpu.SemaphoreType.DMA((len(sources),)),
        ],
        0.001,
        24,
        earlier,
        grid=(width // tile,),
    )(hot, *sources, *acts)


def home_body(experts, cap, cut, row_total, firsts, logits, ids, *refs):
    arrived, back = refs[:experts], refs[experts : 2 * experts]
    extra = refs[2 * experts : 2 * experts + experts // 2]
    grad_rows, grad_logits, norm, pads, table, sems = refs[2 * experts + experts // 2 :]
    copies = [
        pltpu.make_async_copy(
            arrived[m].at[pl.ds(firsts[m], 16), pl.ds(arrived[m].shape[1] - LANES, LANES)],
            pads.at[pl.ds(16 * m, 16), :],
            sems.at[m],
        )
        for m in range(experts)
    ]
    for copy in copies:
        copy.start()
    onehot, spread = routing(ids[...], lax.axis_index("expert"), cap, experts)
    slots = (experts + 1) * cap
    for m in range(experts):
        table[m * cap : (m + 1) * cap, :] = back[m][...]
    over = extra[0][...]
    for piece in extra[1:]:
        over = over + piece[...]
    table[experts * cap :, :] = over
    lane = lane_iota((8, LANES))
    square = tree([back[m][0:16, cut:].astype(F32)[0:8] for m in range(experts)])
    square = jnp.where((lane >= SQUARE_LANE) & (lane < SQUARE_LANE + 3), square, 0.0)
    norm[0] = jnp.max(jnp.sqrt(jnp.sum(square, axis=1, keepdims=True)))
    pick = spread.T[:, :slots].astype(BF16)
    grad_rows[...] = jnp.dot(pick, table[:, :cut], preferred_element_type=F32).astype(BF16)
    gate_rows = jnp.dot(pick, table[:, cut:], preferred_element_type=F32).T[0:1]
    for copy in copies:
        copy.wait()
    counts = jnp.zeros((1, LANES), F32)
    for m in range(experts):
        counts = counts + pads[16 * m : 16 * m + 16, :].astype(F32)[0:1]
    counts = jnp.broadcast_to(counts, (8, LANES)).T[COUNT_LANE : COUNT_LANE + experts, 0:1]
    probs = softmax(logits[...])
    pulls = onehot * gate_rows + aux_weight * experts * (counts / row_total)
    grad_logits[...] = probs * (pulls - jnp.sum(probs * pulls, axis=0, keepdims=True))


def home(logits, ids, arrived, back, extra, cap, row_total):
    experts = len(back)
    rows = ids.shape[1]
    cut = back[0].shape[1] - LANES
    return call(
        functools.partial(
            home_body, experts, cap, cut, row_total, [first for _, first, *_ in arrived]
        ),
        "home",
        [
            jax.ShapeDtypeStruct((rows, cut), BF16),
            jax.ShapeDtypeStruct(logits.shape, F32),
            jax.ShapeDtypeStruct((1,), F32),
        ],
        [VMEM, VMEM] + [ANY] * experts + [VMEM] * (experts + len(extra)),
        [VMEM, VMEM, SMEM],
        [
            pltpu.VMEM((16 * experts, LANES), BF16),
            pltpu.VMEM(((experts + 1) * cap, cut + LANES), BF16),
            pltpu.SemaphoreType.DMA((experts,)),
        ],
        0.001,
        12,
    )(logits, ids, *[piece for piece, *_ in arrived], *back, *extra)


def swap(value, axis, mask):
    size = lax.axis_size(axis)
    return lax.ppermute(value, axis, [(i, i ^ mask) for i in range(size)])


def after(values, done):
    tied = lax.optimization_barrier((*values, *done))
    return tied[: len(values)], tied[len(values) :]


def local(rows_x, rows_dy, router_logits, expert_of, w_gate, w_up, w_down):
    experts = lax.axis_size("expert")
    n_dp = lax.axis_size("dp")
    rows, width = rows_x.shape
    cap = rows // 8
    cut = width // n_dp
    weights = (w_gate[0], w_up[0], w_down[0])
    hidden_units = weights[0].shape[0]
    logits, ids = router_logits.T, expert_of.reshape(1, rows)
    evens = list(range(0, experts, 2))
    near = [m for m in evens[1:] if m & (m - 1) == 0]
    far = [m for m in evens[1:] if m & (m - 1)]
    path = {m: [b for b in near if m & b] for m in far}
    path.update({m ^ 1: [b for b in near[::-1] if m & b] for m in far})
    first_hop = {b: [m for m in path if path[m][0] == b] for b in near}
    plan = [[0], [1, experts, *range(3, experts, 2)], [experts]]
    plan += [[b] + [m for m in first_hop[b] if m % 2 == 0] for b in near]
    own, beside, spare, *mine, part, hot = dispatch(
        rows_x, rows_dy, logits, ids, experts, cap, plan
    )
    bits = [1 << i for i in range(n_dp.bit_length() - 1)]
    token = []

    def step(kernel, *given):
        result = kernel(tuple(token), *given)
        token[:] = [result[-1]]
        return result

    def wait_for(*arrived):
        token.extend(arrived)

    def backward(parts, kind=False, micros=0.001):
        return step(rows_backward, hot, parts, weights, n_dp, kind, micros)

    def turn(pair, bit):
        *kept, sent = pair
        return *kept, swap(sent, "dp", bit)

    def middle(pair):
        for bit in bits[1:]:
            pair = turn(step(fold, pair, cut), bit)
        return pair

    beside = swap(beside, "expert", 1)

    def from_beside(m):
        at = plan[1].index(m) * cap
        return beside[at : at + cap]

    cold = {0: (own, 0, cap, None), 1: (beside, 0, cap, None)}
    chunks = [[0, 1], [m ^ c for c in (0, 1) for m in near], [m ^ c for c in (0, 1) for m in far]]
    over = [swap(part, "expert", m) for m in evens[1:]]
    *first, acts_first = backward([cold[m] for m in chunks[0]])
    over, (acts_first,) = after(over, [acts_first])
    this = jnp.concatenate(over, axis=0)
    that = swap(this, "dp", 1)
    kept, sent = step(fold, turn(first, bits[0]), cut)
    (that,), (sent,) = after([that], [sent])
    first = turn((kept, sent), bits[1])
    for bit in bits[2:]:
        first = turn(step(fold, first, cut), bit)
    count = this.shape[0]
    extras = [(spare, 0, cap, None), (this, 0, count, "this"), (that, 0, count, "that")]
    extras += [(beside, cap, cap, None)]
    extras += [(swap(this, "expert", 1), 0, count, "this")]
    extras += [(swap(that, "expert", 1), 0, count, "that")]
    loads = []
    for b, part in zip(near, mine):
        odd = [b ^ 1] + [m for m in first_hop[b] if m % 2]
        loads.append(jnp.concatenate([part] + [from_beside(m) for m in odd], axis=0))
    loads, (this,) = after(loads, [this])
    loads = [swap(load, "expert", b) for b, load in zip(near, loads)]

    kept, sent, far_kept, far_sent, acts_hot = backward(extras, True)
    far_sent = swap(far_sent, "expert", 1)
    far_kept = swap(far_kept, "expert", 1)
    (sent,) = step(merge, sent, far_sent)
    passed = {}
    for b, load in zip(near, loads):
        items = [b] + [m for m in first_hop[b] if m % 2 == 0]
        items += [b ^ 1] + [m for m in first_hop[b] if m % 2]
        for i, m in enumerate(items):
            if m in path:
                passed[m] = load[i * cap : (i + 1) * cap]
            else:
                cold[m] = (load, i * cap, cap, None)
    on_way = list(passed)
    parts, (sent,) = after([passed[m] for m in on_way], [sent])
    for m, part in zip(on_way, parts):
        for b in path[m][1:]:
            part = swap(part, "expert", b)
        cold[m] = (part, 0, cap, None)
    busy = turn((kept, far_kept, sent), bits[0])
    *second, acts_second = backward([cold[m] for m in chunks[1]])
    second = turn(second, bits[0])
    busy = middle(busy)
    *third, acts_third = backward([cold[m] for m in chunks[2]])
    third = turn(third, bits[0])
    grad_gate, grad_up, grad_down, squares = step(
        weights_backward,
        hot,
        [cold[m] for m in sum(chunks, [])],
        extras,
        [acts_first, acts_second, acts_third, acts_hot],
        hidden_units,
        width,
    )
    wait_for(busy[-1], first[-1])
    second = middle(second)
    for bit in bits[1:]:
        kept, sent = step(fold, third, cut)
        (squares,), (sent,) = after([squares], [sent])
        third = turn((kept, sent), bit)
    squares = [squares] + [swap(squares, "dp", m) for m in range(1, n_dp)]
    over_back = step(last, [], [busy], [evens], evens, cut, cap)
    over_back = [piece if m == 0 else swap(piece, "expert", m) for m, piece in zip(evens, over_back)]
    wait_for(*over_back[1:])
    back = {}
    for masks, given, where in (
        (chunks[0] + chunks[1], [first, second], chunks[:2]),
        (chunks[2], [third], chunks[2:]),
    ):
        for m, piece in zip(masks, step(last, squares, given, where, masks, cut, cap)):
            back[m] = piece if m == 0 else swap(piece, "expert", m)
    grad_rows, grad_logits, norm = home(
        logits,
        ids,
        [cold[m] for m in range(experts)],
        [back[m] for m in range(experts)],
        over_back,
        cap,
        rows * experts,
    )
    return (
        grad_rows,
        grad_logits.T,
        grad_gate[None],
        grad_up[None],
        grad_down[None],
        norm.reshape(()),
    )


def solution(mesh):
    in_specs = (
        P("expert", None),
        P("expert", None),
        P("expert", None),
        P("expert", None),
        P("expert", "dp", None),
        P("expert", "dp", None),
        P("expert", "dp", None),
    )
    out_specs = (
        P("expert", "dp"),
        P("expert", None),
        P("expert", "dp", None),
        P("expert", "dp", None),
        P("expert", "dp", None),
        P(),
    )
    return jax.shard_map(local, mesh=mesh, in_specs=in_specs, out_specs=out_specs, check_vma=False)
```

```python
import functools

import jax
import jax.numpy as jnp
from jax import lax
from jax.experimental import pallas as pl
from jax.experimental.pallas import tpu as pltpu
from jax.sharding import PartitionSpec as P

aux_weight = 1.0
LANES = 128
COUNT_LANE = 64
RATE = 1e9
SQUARE_LANE = 8
BF16 = jnp.bfloat16
F32 = jnp.float32
ANY = pl.BlockSpec(memory_space=pl.ANY)
VMEM = pl.BlockSpec(memory_space=pltpu.VMEM)
SMEM = pl.BlockSpec(memory_space=pltpu.SMEM)
HBM = pl.BlockSpec(memory_space=pltpu.HBM)


def call(body, name, out_shape, in_specs, out_specs, scratch, micros, room, earlier=(), **extra):
    skipped = len(earlier)

    def without(*refs):
        body(*refs[skipped:])

    kernel = pl.pallas_call(
        without,
        name=name,
        out_shape=out_shape,
        in_specs=[ANY] * skipped + in_specs,
        out_specs=out_specs,
        scratch_shapes=scratch,
        cost_estimate=pl.CostEstimate(
            flops=int(micros * RATE), bytes_accessed=1000, transcendentals=0
        ),
        compiler_params=pltpu.CompilerParams(vmem_limit_bytes=room * 1024 * 1024),
        **extra,
    )
    return functools.partial(kernel, *earlier)


def lane_iota(shape):
    return lax.broadcasted_iota(jnp.int32, shape, len(shape) - 1)


def routing(ids, me, cap, experts):
    rows = ids.shape[1]
    expert = lax.broadcasted_iota(jnp.int32, (experts, rows), 0)
    onehot = jnp.where(expert == ids, 1.0, 0.0)
    before = lax.broadcasted_iota(jnp.int32, (rows, rows), 0) < lane_iota((rows, rows))
    earlier = jnp.dot(
        onehot.astype(BF16), jnp.where(before, 1.0, 0.0).astype(BF16), preferred_element_type=F32
    )
    rank = jnp.sum(earlier * onehot, axis=0, keepdims=True).astype(jnp.int32)
    slot = jnp.where(rank < cap, (ids ^ me) * cap + rank, experts * cap + rank - cap)
    slots = -(-(experts + 1) * cap // LANES) * LANES
    spread = lax.broadcasted_iota(jnp.int32, (slots, rows), 0) == slot
    return onehot, jnp.where(spread, 1.0, 0.0)


def softmax(logits):
    scores = jnp.exp(logits - jnp.max(logits, axis=0, keepdims=True))
    return scores / jnp.sum(scores, axis=0, keepdims=True)


def dispatch_body(plan, experts, cap, width, x_hbm, dy_hbm, logits_hbm, ids_hbm, *refs):
    outs, part, hot = refs[: len(plan)], refs[len(plan)], refs[len(plan) + 1]
    held, logits, ids, sems = refs[len(plan) + 2 :]
    loads = [
        pltpu.make_async_copy(ids_hbm, ids, sems.at[0]),
        pltpu.make_async_copy(logits_hbm, logits, sems.at[1]),
        pltpu.make_async_copy(x_hbm, held.at[0], sems.at[2]),
        pltpu.make_async_copy(dy_hbm, held.at[1], sems.at[3]),
    ]
    for load in loads:
        load.start()
    me = lax.axis_index("expert")
    slots = (experts + 1) * cap
    loads[0].wait()
    loads[1].wait()
    expert_ids = ids[...]
    onehot, spread = routing(expert_ids, me, cap, experts)
    spread = spread[:slots]
    gate = jnp.sum(softmax(logits[...]) * onehot, axis=0, keepdims=True)
    gate = gate.astype(BF16).astype(F32)
    mine = jnp.sum(jnp.where(expert_ids == me, 1, 0))
    hot[0] = jnp.where(mine > cap, 1, 0)
    counts = jnp.sum(onehot, axis=1, keepdims=True)
    expert = lax.broadcasted_iota(jnp.int32, (experts, LANES), 0)
    counts = jnp.sum(
        jnp.where(lane_iota((experts, LANES)) - COUNT_LANE == expert, counts, 0.0),
        axis=0,
        keepdims=True,
    )
    gates = jnp.sum(spread * gate, axis=1, keepdims=True)
    pad = jnp.where(lane_iota((slots, LANES)) == 0, gates, counts).astype(BF16)
    places = [(m, outs[i], j * cap) for i, held_by in enumerate(plan) for j, m in enumerate(held_by)]
    for m, out, first in places:
        out[first : first + cap, 2 * width :] = pad[m * cap : (m + 1) * cap]
    part[:, width:] = pad[experts * cap :]
    parity = lax.rem(lax.axis_index("dp"), 2)
    spread = spread.astype(BF16)
    tile = 1024
    for half in range(2):
        loads[2 + half].wait()
        for at in range(0, width, tile):
            moved = jnp.dot(
                spread, held[half, :, at : at + tile], preferred_element_type=F32
            ).astype(BF16)
            for m, out, first in places:
                out[first : first + cap, half * width + at : half * width + at + tile] = moved[
                    m * cap : (m + 1) * cap
                ]

            @pl.when(parity == half)
            def _():
                part[:, at : at + tile] = moved[experts * cap :]


def dispatch(rows_x, rows_dy, logits, ids, experts, cap, plan):
    rows, width = rows_x.shape
    wide = 2 * width + LANES
    return call(
        functools.partial(dispatch_body, plan, experts, cap, width),
        "dispatch",
        [jax.ShapeDtypeStruct((len(held_by) * cap, wide), BF16) for held_by in plan]
        + [jax.ShapeDtypeStruct((cap, width + LANES), BF16)]
        + [jax.ShapeDtypeStruct((1,), jnp.int32)],
        [HBM] * 4,
        [VMEM] * (len(plan) + 1) + [SMEM],
        [
            pltpu.VMEM((2, rows, width), BF16),
            pltpu.VMEM(logits.shape, F32),
            pltpu.VMEM(ids.shape, jnp.int32),
            pltpu.SemaphoreType.DMA((4,)),
        ],
        6,
        58,
    )(rows_x, rows_dy, logits, ids)


def split_lanes(total):
    lane = lane_iota((total.shape[0], LANES))
    first = total.astype(BF16).astype(F32)
    second = (total - first).astype(BF16).astype(F32)
    third = total - first - second
    return jnp.where(
        lane == 0, first, jnp.where(lane == 1, second, jnp.where(lane == 2, third, 0.0))
    ).astype(BF16)


def moves(ranges, width, extra):
    parity = lax.rem(lax.axis_index("dp"), 2)
    found, at = [], 0
    for p, (first, count, side) in enumerate(ranges):
        if side is None:
            found.append((p, first, count, 0, 2 * width + extra, at, 0))
        elif side == "this":
            found.append((p, first, count, 0, width, at, pl.multiple_of(parity * width, width)))
            if extra:
                found.append((p, first, count, width, extra, at, 2 * width))
        else:
            at -= count
            column = pl.multiple_of((1 - parity) * width, width)
            found.append((p, first, count, 0, width, at, column))
        at += count
    return found


def rows_in(ranges):
    return sum(count for _, count, side in ranges if side != "that")


def rows_body(ranges, width, n_dp, guarded, hot, *refs):
    pieces = len(ranges)
    sources, weights = refs[:pieces], refs[pieces : pieces + 3]
    outs = refs[pieces + 3 : -2]
    held, piece_sems = refs[-2:]
    hidden_units = weights[0].shape[0]
    rows = held.shape[0]

    def work():
        copies = [
            pltpu.make_async_copy(
                sources[p].at[pl.ds(first, count), pl.ds(column, columns)],
                held.at[pl.ds(at, count), pl.ds(target, columns)],
                piece_sems.at[i],
            )
            for i, (p, first, count, column, columns, at, target) in enumerate(
                moves(ranges, width, LANES)
            )
        ]
        for copy in copies:
            copy.start()
        for copy in copies:
            copy.wait()
        pre_gate, pre_up, grad = [
            lax.dot_general(
                held[:, side * width : (side + 1) * width],
                weight[...],
                (((1,), (1,)), ((), ())),
                preferred_element_type=F32,
            )
            for side, weight in zip((0, 0, 1), weights)
        ]
        gate = held[:, 2 * width :].astype(F32)[:, 0:1]
        sigmoid = jax.nn.sigmoid(pre_gate)
        active = pre_gate * sigmoid
        hidden = (active * pre_up).astype(BF16)
        hidden_f = hidden.astype(F32)
        gate_part = jnp.sum(hidden_f * grad, axis=1, keepdims=True)
        grad_hidden = grad * gate
        d_up = (grad_hidden * active).astype(BF16)
        d_pre = (grad_hidden * pre_up * sigmoid * (1.0 + pre_gate * (1.0 - sigmoid))).astype(BF16)
        outs[-1][:, :hidden_units] = d_pre
        outs[-1][:, hidden_units : 2 * hidden_units] = d_up
        outs[-1][:, 2 * hidden_units :] = (hidden_f * gate).astype(BF16)
        lanes = split_lanes(gate_part)
        cut = width // n_dp
        part = n_dp // 2 * cut + LANES
        me = lax.axis_index("dp")
        for half in range(2):
            places = [(outs[half], 0)]
            if guarded:
                places.append((outs[2 + half], rows // 2))
            for out, first in places:
                count = out.shape[0]
                out[:, part - LANES :] = lanes[first : first + count]
                for p in range(n_dp // 2):
                    column = pl.multiple_of((me ^ (2 * p + half)) * cut, cut)
                    out[:, p * cut : (p + 1) * cut] = (
                        jnp.dot(
                            d_pre[first : first + count],
                            weights[0][:, pl.ds(column, cut)],
                            preferred_element_type=F32,
                        )
                        + jnp.dot(
                            d_up[first : first + count],
                            weights[1][:, pl.ds(column, cut)],
                            preferred_element_type=F32,
                        )
                    ).astype(BF16)

    if guarded:

        @pl.when(hot[0] == 1)
        def _():
            work()

        @pl.when(hot[0] != 1)
        def _():
            for out in outs:
                out[...] = jnp.zeros_like(out)
    else:
        work()


def rows_backward(earlier, hot, parts, weights, n_dp, guarded, micros=0.001):
    width = weights[0].shape[1]
    hidden_units = weights[0].shape[0]
    sources = [source for source, *_ in parts]
    ranges = [tuple(where) for _, *where in parts]
    rows = rows_in(ranges)
    part = width // 2 + LANES
    shapes = [(rows // 2, part)] * 4 if guarded else [(rows, part)] * 2
    return call(
        functools.partial(rows_body, ranges, width, n_dp, guarded),
        "rows_backward",
        [jax.ShapeDtypeStruct(s, BF16) for s in shapes]
        + [jax.ShapeDtypeStruct((rows, 3 * hidden_units), BF16)],
        [SMEM] + [ANY] * len(sources) + [VMEM] * 3,
        [VMEM] * (len(shapes) + 1),
        [
            pltpu.VMEM((rows, 2 * width + LANES), BF16),
            pltpu.SemaphoreType.DMA((2 * len(sources),)),
        ],
        micros,
        20,
        earlier,
    )(hot, *sources, *weights)


def merge_body(own, peers, out):
    out[...] = own[...] + peers[...]


def merge(earlier, own, peers):
    return call(
        merge_body,
        "merge",
        [jax.ShapeDtypeStruct(own.shape, BF16)],
        [VMEM] * 2,
        [VMEM],
        [],
        0.001,
        8,
        earlier,
    )(own, peers)


def sum_of(parts, columns):
    return functools.reduce(jnp.add, [part[:, columns].astype(F32) for part in parts])


def fold_body(cut, parts, count, *refs):
    given, outs = refs[:count], refs[count:]
    total = sum_of(given, slice(parts * cut, None))
    lanes = split_lanes(jnp.sum(total, axis=1, keepdims=True))
    for out in outs:
        out[:, parts // 2 * cut :] = lanes
    for p in range(parts):
        columns = slice(p * cut, (p + 1) * cut)
        outs[p % 2][:, p // 2 * cut : (p // 2 + 1) * cut] = sum_of(given, columns).astype(BF16)


def fold(earlier, given, cut):
    rows = given[0].shape[0]
    parts = (given[0].shape[1] - LANES) // cut
    shape = jax.ShapeDtypeStruct((rows, parts // 2 * cut + LANES), BF16)
    return call(
        functools.partial(fold_body, cut, parts, len(given)),
        "fold",
        [shape] * 2,
        [VMEM] * len(given),
        [VMEM] * 2,
        [],
        0.001,
        8,
        earlier,
    )(*given)


def tree(values):
    while len(values) > 1:
        values = [a + b for a, b in zip(values[::2], values[1::2])]
    return values[0]


def last_body(cut, cap, places, count, *refs):
    pairs = len(places)
    squares, given, outs = refs[:count], refs[count : count + 2 * pairs], refs[count + 2 * pairs :]
    total = tree([part[0:1, 0:1] for part in squares]) if squares else jnp.zeros((1, 1), F32)
    lane = lane_iota((1, LANES))
    square = jnp.zeros((1, LANES), F32)
    for i in range(3):
        part = total.astype(BF16).astype(F32)
        square = jnp.where(lane == SQUARE_LANE + i, part, square)
        total = total - part
    for i, where in enumerate(places):
        pair = given[2 * i : 2 * i + 2]
        whole = sum_of(pair, slice(0, cut)).astype(BF16)
        gates = jnp.sum(sum_of(pair, slice(cut, None)), axis=1, keepdims=True)
        lanes = jnp.where(lane == 0, gates, square).astype(BF16)
        for start, out in where:
            outs[out][:, :cut] = whole[start : start + cap]
            outs[out][:, cut:] = lanes[start : start + cap]


def last(earlier, squares, pairs, chunks, masks, cut, cap):
    places = [[(j * cap, masks.index(m)) for j, m in enumerate(chunk)] for chunk in chunks]
    return call(
        functools.partial(last_body, cut, cap, places, len(squares)),
        "last",
        [jax.ShapeDtypeStruct((cap, cut + LANES), BF16)] * len(masks),
        [VMEM] * (len(squares) + 2 * len(pairs)),
        [VMEM] * len(masks),
        [],
        0.001,
        12,
        earlier,
    )(*squares, *[part for pair in pairs for part in pair])


def weights_body(ranges, cold_pieces, acts_count, width, tile, hot, *refs):
    pieces = len(ranges)
    sources, acts = refs[:pieces], refs[pieces : pieces + acts_count]
    outs, squares = refs[pieces + acts_count : -4][:3], refs[pieces + acts_count : -4][3]
    held, factors, total, sems = refs[-4:]
    step = pl.program_id(0)
    hidden_units = outs[0].shape[0]


    def copies(count):
        return [
            pltpu.make_async_copy(
                sources[p].at[pl.ds(first, size), pl.ds(column, columns)],
                held.at[pl.ds(at, size), pl.ds(target, columns)],
                sems.at[p],
            )
            for p, first, size, column, columns, at, target in moves(ranges, width, 0)
            if p in count
        ]

    @pl.when(step == 0)
    def _():
        for copy in copies(range(cold_pieces)):
            copy.start()

        @pl.when(hot[0] == 1)
        def _():
            for copy in copies(range(cold_pieces, pieces)):
                copy.start()

        at = 0
        for act in acts:
            factors[:, at : at + act.shape[0]] = act[...].astype(F32).T.astype(BF16)
            at += act.shape[0]
        total[...] = jnp.zeros_like(total)
        for copy in copies(range(cold_pieces)):
            copy.wait()

        @pl.when(hot[0] == 1)
        def _():
            for copy in copies(range(cold_pieces, pieces)):
                copy.wait()

    def work(rows):
        for i in range(3):
            at = pl.multiple_of((width if i == 2 else 0) + step * tile, tile)
            gradient = jnp.dot(
                factors[i * hidden_units : (i + 1) * hidden_units, :rows],
                held[:rows, pl.ds(at, tile)],
                preferred_element_type=F32,
            )
            outs[i][...] = gradient
            total[...] += jnp.sum((gradient * gradient).reshape(-1, 8, tile), axis=0)

    @pl.when(hot[0] == 1)
    def _():
        work(rows_in(ranges))

    @pl.when(hot[0] != 1)
    def _():
        work(rows_in(ranges[:cold_pieces]))

    @pl.when(step == pl.num_programs(0) - 1)
    def _():
        squares[...] = jnp.full(squares.shape, jnp.sum(total[...]), F32)


def weights_backward(earlier, hot, cold, extra, acts, hidden_units, width):
    tile = 512
    sources = [source for source, *_ in cold + extra]
    ranges = [tuple(where) for _, *where in cold + extra]
    rows = rows_in(ranges)
    block = pl.BlockSpec((hidden_units, tile), lambda j: (0, j))
    whole = [pl.BlockSpec(a.shape, lambda j: (0, 0)) for a in acts]
    return call(
        functools.partial(
            weights_body, ranges, len(cold), len(acts), width, tile
        ),
        "weights_backward",
        [jax.ShapeDtypeStruct((hidden_units, width), F32)] * 3
        + [jax.ShapeDtypeStruct((8, LANES), F32)],
        [SMEM] + [ANY] * len(sources) + whole,
        [block] * 3 + [pl.BlockSpec((8, LANES), lambda j: (0, 0))],
        [
            pltpu.VMEM((rows, 2 * width), BF16),
            pltpu.VMEM((3 * hidden_units, rows), BF16),
            pltpu.VMEM((8, tile), F32),
            pltpu.SemaphoreType.DMA((len(sources),)),
        ],
        0.001,
        24,
        earlier,
        grid=(width // tile,),
    )(hot, *sources, *acts)


def home_body(experts, cap, cut, row_total, firsts, logits, ids, *refs):
    arrived, back = refs[:experts], refs[experts : 2 * experts]
    extra = refs[2 * experts : 2 * experts + experts // 2]
    grad_rows, grad_logits, norm, pads, table, sems = refs[2 * experts + experts // 2 :]
    copies = [
        pltpu.make_async_copy(
            arrived[m].at[pl.ds(firsts[m], 16), pl.ds(arrived[m].shape[1] - LANES, LANES)],
            pads.at[pl.ds(16 * m, 16), :],
            sems.at[m],
        )
        for m in range(experts)
    ]
    for copy in copies:
        copy.start()
    onehot, spread = routing(ids[...], lax.axis_index("expert"), cap, experts)
    slots = (experts + 1) * cap
    for m in range(experts):
        table[m * cap : (m + 1) * cap, :] = back[m][...]
    over = extra[0][...]
    for piece in extra[1:]:
        over = over + piece[...]
    table[experts * cap :, :] = over
    lane = lane_iota((8, LANES))
    square = tree([back[m][0:16, cut:].astype(F32)[0:8] for m in range(experts)])
    square = jnp.where((lane >= SQUARE_LANE) & (lane < SQUARE_LANE + 3), square, 0.0)
    norm[0] = jnp.max(jnp.sqrt(jnp.sum(square, axis=1, keepdims=True)))
    pick = spread.T[:, :slots].astype(BF16)
    grad_rows[...] = jnp.dot(pick, table[:, :cut], preferred_element_type=F32).astype(BF16)
    gate_rows = jnp.dot(pick, table[:, cut:], preferred_element_type=F32).T[0:1]
    for copy in copies:
        copy.wait()
    counts = jnp.zeros((1, LANES), F32)
    for m in range(experts):
        counts = counts + pads[16 * m : 16 * m + 16, :].astype(F32)[0:1]
    counts = jnp.broadcast_to(counts, (8, LANES)).T[COUNT_LANE : COUNT_LANE + experts, 0:1]
    probs = softmax(logits[...])
    pulls = onehot * gate_rows + aux_weight * experts * (counts / row_total)
    grad_logits[...] = probs * (pulls - jnp.sum(probs * pulls, axis=0, keepdims=True))


def home(logits, ids, arrived, back, extra, cap, row_total):
    experts = len(back)
    rows = ids.shape[1]
    cut = back[0].shape[1] - LANES
    return call(
        functools.partial(
            home_body, experts, cap, cut, row_total, [first for _, first, *_ in arrived]
        ),
        "home",
        [
            jax.ShapeDtypeStruct((rows, cut), BF16),
            jax.ShapeDtypeStruct(logits.shape, F32),
            jax.ShapeDtypeStruct((1,), F32),
        ],
        [VMEM, VMEM] + [ANY] * experts + [VMEM] * (experts + len(extra)),
        [VMEM, VMEM, SMEM],
        [
            pltpu.VMEM((16 * experts, LANES), BF16),
            pltpu.VMEM(((experts + 1) * cap, cut + LANES), BF16),
            pltpu.SemaphoreType.DMA((experts,)),
        ],
        0.001,
        12,
    )(logits, ids, *[piece for piece, *_ in arrived], *back, *extra)


def swap(value, axis, mask):
    size = lax.axis_size(axis)
    return lax.ppermute(value, axis, [(i, i ^ mask) for i in range(size)])


def after(values, done):
    tied = lax.optimization_barrier((*values, *done))
    return tied[: len(values)], tied[len(values) :]


def local(rows_x, rows_dy, router_logits, expert_of, w_gate, w_up, w_down):
    experts = lax.axis_size("expert")
    n_dp = lax.axis_size("dp")
    rows, width = rows_x.shape
    cap = rows // 8
    cut = width // n_dp
    weights = (w_gate[0], w_up[0], w_down[0])
    hidden_units = weights[0].shape[0]
    logits, ids = router_logits.T, expert_of.reshape(1, rows)
    evens = list(range(0, experts, 2))
    near = [m for m in evens[1:] if m & (m - 1) == 0]
    far = [m for m in evens[1:] if m & (m - 1)]
    path = {m: [b for b in near if m & b] for m in far}
    path.update({m ^ 1: [b for b in near[::-1] if m & b] for m in far})
    first_hop = {b: [m for m in path if path[m][0] == b] for b in near}
    plan = [[0], [1, experts, *range(3, experts, 2)], [experts]]
    plan += [[b] + [m for m in first_hop[b] if m % 2 == 0] for b in near]
    own, beside, spare, *mine, part, hot = dispatch(
        rows_x, rows_dy, logits, ids, experts, cap, plan
    )
    bits = [1 << i for i in range(n_dp.bit_length() - 1)]
    token = []

    def step(kernel, *given):
        result = kernel(tuple(token), *given)
        token[:] = [result[-1]]
        return result

    def wait_for(*arrived):
        token.extend(arrived)

    def backward(parts, kind=False, micros=0.001):
        return step(rows_backward, hot, parts, weights, n_dp, kind, micros)

    def turn(pair, bit):
        *kept, sent = pair
        return *kept, swap(sent, "dp", bit)

    def middle(pair):
        for bit in bits[1:]:
            pair = turn(step(fold, pair, cut), bit)
        return pair

    beside = swap(beside, "expert", 1)

    def from_beside(m):
        at = plan[1].index(m) * cap
        return beside[at : at + cap]

    cold = {0: (own, 0, cap, None), 1: (beside, 0, cap, None)}
    chunks = [[0, 1], [m ^ c for c in (0, 1) for m in near], [m ^ c for c in (0, 1) for m in far]]
    over = [swap(part, "expert", m) for m in evens[1:]]
    *first, acts_first = backward([cold[m] for m in chunks[0]])
    over, (acts_first,) = after(over, [acts_first])
    this = jnp.concatenate(over, axis=0)
    that = swap(this, "dp", 1)
    kept, sent = step(fold, turn(first, bits[0]), cut)
    (that,), (sent,) = after([that], [sent])
    first = turn((kept, sent), bits[1])
    for bit in bits[2:]:
        first = turn(step(fold, first, cut), bit)
    count = this.shape[0]
    extras = [(spare, 0, cap, None), (this, 0, count, "this"), (that, 0, count, "that")]
    extras += [(beside, cap, cap, None)]
    extras += [(swap(this, "expert", 1), 0, count, "this")]
    extras += [(swap(that, "expert", 1), 0, count, "that")]
    loads = []
    for b, part in zip(near, mine):
        odd = [b ^ 1] + [m for m in first_hop[b] if m % 2]
        loads.append(jnp.concatenate([part] + [from_beside(m) for m in odd], axis=0))
    loads, (this,) = after(loads, [this])
    loads = [swap(load, "expert", b) for b, load in zip(near, loads)]

    kept, sent, far_kept, far_sent, acts_hot = backward(extras, True)
    far_sent = swap(far_sent, "expert", 1)
    far_kept = swap(far_kept, "expert", 1)
    (sent,) = step(merge, sent, far_sent)
    passed = {}
    for b, load in zip(near, loads):
        items = [b] + [m for m in first_hop[b] if m % 2 == 0]
        items += [b ^ 1] + [m for m in first_hop[b] if m % 2]
        for i, m in enumerate(items):
            if m in path:
                passed[m] = load[i * cap : (i + 1) * cap]
            else:
                cold[m] = (load, i * cap, cap, None)
    on_way = list(passed)
    parts, (sent,) = after([passed[m] for m in on_way], [sent])
    for m, part in zip(on_way, parts):
        for b in path[m][1:]:
            part = swap(part, "expert", b)
        cold[m] = (part, 0, cap, None)
    busy = turn((kept, far_kept, sent), bits[0])
    *second, acts_second = backward([cold[m] for m in chunks[1]])
    second = turn(second, bits[0])
    busy = middle(busy)
    *third, acts_third = backward([cold[m] for m in chunks[2]])
    third = turn(third, bits[0])
    grad_gate, grad_up, grad_down, squares = step(
        weights_backward,
        hot,
        [cold[m] for m in sum(chunks, [])],
        extras,
        [acts_first, acts_second, acts_third, acts_hot],
        hidden_units,
        width,
    )
    wait_for(busy[-1], first[-1])
    second = middle(second)
    over_back = step(last, [], [busy], [evens], evens, cut, cap)
    over_back = [piece if m == 0 else swap(piece, "expert", m) for m, piece in zip(evens, over_back)]
    wait_for(*over_back[1:])
    for bit in bits[1:]:
        kept, sent = step(fold, third, cut)
        (squares,), (sent,) = after([squares], [sent])
        third = turn((kept, sent), bit)
    squares = [squares] + [swap(squares, "dp", m) for m in range(1, n_dp)]
    back = {}
    for masks, given, where in (
        (chunks[0] + chunks[1], [first, second], chunks[:2]),
        (chunks[2], [third], chunks[2:]),
    ):
        for m, piece in zip(masks, step(last, squares, given, where, masks, cut, cap)):
            back[m] = piece if m == 0 else swap(piece, "expert", m)
    grad_rows, grad_logits, norm = home(
        logits,
        ids,
        [cold[m] for m in range(experts)],
        [back[m] for m in range(experts)],
        over_back,
        cap,
        rows * experts,
    )
    return (
        grad_rows,
        grad_logits.T,
        grad_gate[None],
        grad_up[None],
        grad_down[None],
        norm.reshape(()),
    )


def solution(mesh):
    in_specs = (
        P("expert", None),
        P("expert", None),
        P("expert", None),
        P("expert", None),
        P("expert", "dp", None),
        P("expert", "dp", None),
        P("expert", "dp", None),
    )
    out_specs = (
        P("expert", "dp"),
        P("expert", None),
        P("expert", "dp", None),
        P("expert", "dp", None),
        P("expert", "dp", None),
        P(),
    )
    return jax.shard_map(local, mesh=mesh, in_specs=in_specs, out_specs=out_specs, check_vma=False)
```
